512 devices in a mesh: dp: 8 (over z), tm: 8 (over y_lo, core), height: 8 (over x, y_hi).
Axes of the slice: x: 4, y: 8 (y_hi: 2, y_lo: 4; y = y_hi * 4 + y_lo), z: 8, core: 2. Of those that a mesh axis runs over, the one named last changes fastest.
Arguments:
- clip_inputs: bfloat16 [8, 16, 16, 16, 512], P('dp', 'tm', 'height'), may hold values from -6 to 6
- conv_in_weight: bfloat16 [13824, 512], P(('tm', 'height'), 'dp'), may hold values from -0.0546875 to 0.0546875
- group_gain: bfloat16 [512], P('dp'), may hold values from 0.099609375 to 1.8984375
- group_bias: bfloat16 [512], P('dp'), may hold values from -3 to 3
- conv_out_weight: bfloat16 [27, 512, 16], P(None, 'dp'), may hold values from -0.109375 to 0.109375
- out_bias: float32 [16], replicated, may hold values from -3 to 3
- patch_weight: bfloat16 [64, 3072], replicated, may hold values from -1.5 to 1.5
- patch_bias: bfloat16 [3072], replicated, may hold values from -3 to 3
- qkv_weight: bfloat16 [3072, 6144], P(('tm', 'height'), 'dp'), may hold values from -0.109375 to 0.109375
- qkv_bias: bfloat16 [6144], P('dp'), may hold values from -3 to 3
- q_gain: bfloat16 [128], replicated, may hold values from 0.099609375 to 1.8984375
- k_gain: bfloat16 [128], replicated, may hold values from 0.099609375 to 1.8984375
- frame_pos: int32 [16], P('tm'), may hold values from 0 to 63
- row_pos: int32 [8], P('height'), may hold values from 0 to 127
Outputs:
- latents: float32 [8, 16, 16, 256], P('dp', 'tm', 'height')
- queries: bfloat16 [8, 16, 8, 8, 2048], P(None, 'tm', 'height', None, 'dp')
- keys: bfloat16 [8, 16, 8, 8, 2048], P(None, 'tm', 'height', None, 'dp')
- values: bfloat16 [8, 16, 8, 8, 2048], P(None, 'tm', 'height', None, 'dp')
The draws below stay inside these ranges and needn't reach their ends.
All inputs are finite; a program needn't handle non-finite values.
Results may differ from the reference program's by a relative error of at most 0.01.
Values may be sent and summed in bfloat16 or wider, within the bound.
A program may use at most 64 MiB of HBM per device.

```python
import math
import jax
import jax.numpy as jnp
from jax import lax

C = 512
ZC = 16
HID = 3072
HD = 128
GROUPS = 32
TAPS = 27
COLS = 16
HEADS = 16
CLIPS = 8
FRAMES = 16
ROWS = 16
TROWS = 8
TCOLS = 8
PATCH = 64


def wave_sum(base, freqs, phases, channel_vecs, amplitude):
    frames_at = jnp.arange(FRAMES, dtype=jnp.float32) / FRAMES
    rows_at = jnp.arange(ROWS, dtype=jnp.float32) / ROWS
    cols_at = jnp.arange(COLS, dtype=jnp.float32) / COLS
    total = base
    for mode in range(2):
        argument = 2.0 * math.pi * (freqs[mode, 0] * frames_at[:, None, None] + freqs[mode, 1] * rows_at[None, :, None] + freqs[mode, 2] * cols_at[None, None, :])
        wave = jnp.cos(argument[None] + phases[:, mode][:, None, None, None])
        total = total + amplitude * wave[..., None] * channel_vecs[mode][None, None, None, None, :]
    return total


def draw_clip_inputs(key, part):
    key = jax.random.fold_in(key, 11)
    freq_key, phase_key, chan_key, sign_key, offset_key, noise_key = jax.random.split(key, 6)
    shape = (CLIPS, FRAMES, ROWS, COLS, C)
    freqs = jax.random.randint(freq_key, (2, 3), 1, 4).astype(jnp.float32)
    phases = jax.random.uniform(phase_key, (CLIPS, 2), jnp.float32, -math.pi, math.pi)
    channel_vecs = jnp.clip(jax.random.normal(chan_key, (2, C), jnp.float32), -2.5, 2.5)
    signs = (2 * jax.random.randint(sign_key, (CLIPS,), 0, 2) - 1).astype(jnp.float32)
    offsets = jnp.clip(jax.random.normal(offset_key, (C,), jnp.float32), -2.5, 2.5)
    noise = 0.5 * jnp.clip(jax.random.normal(noise_key, shape, jnp.float32), -3.5, 3.5)
    field = wave_sum(noise, freqs, phases, channel_vecs, 0.7)
    field = field + 0.5 * signs[:, None, None, None, None] * offsets
    return jnp.clip(field, -6.0, 6.0).astype(jnp.bfloat16)


def plant(drawn, stream_key, least, high):
    longest = drawn.shape.index(max(drawn.shape))
    spots = []
    for shift in (0, 1):
        where = [jax.random.randint(jax.random.fold_in(stream_key, axis), (), 0, length) for axis, length in enumerate(drawn.shape)]
        where[longest] = (where[longest] + shift) % drawn.shape[longest]
        spots.append(tuple(where))
    return drawn.at[spots[0]].set(least).at[spots[1]].set(high)


def shard_levels(rng, shape, pieces, least, high):
    def one(position, parts):
        heights = jax.random.uniform(jax.random.fold_in(jax.random.fold_in(rng, 6), position), (parts,), jnp.float32, least / len(pieces), high / len(pieces))
        return jnp.repeat(jnp.exp(heights), shape[position] // parts).reshape((-1,) + (1,) * (len(shape) - position - 1))

    level = one(*pieces[0])
    for cut in pieces[1:]:
        level = level * one(*cut)
    return level


def normal_values(key, shape, deviation, reach, pieces=(), held_as=jnp.bfloat16):
    values = deviation * jax.random.normal(key, shape, jnp.float32)
    if pieces:
        values = values * shard_levels(key, shape, pieces, -0.22, 0.18)
    return jnp.clip(values, -reach, reach).astype(held_as)


def setup_inputs(seed: int = 0) -> dict:
    streams_of = jax.random.split(jax.random.key(seed), 15)
    return {
        "clip_inputs": draw_clip_inputs(jax.random.fold_in(streams_of[14], 71), 0),
        "conv_in_weight": normal_values(streams_of[1], (TAPS * C, C), (TAPS * C) ** -0.5, 0.0546875, ((0, 64), (1, 8))),
        "group_gain": jnp.clip(1.0 + 0.18 * jax.random.normal(streams_of[2], (C,), jnp.float32), 0.099609375, 1.8984375).astype(jnp.bfloat16),
        "group_bias": normal_values(streams_of[3], (C,), 0.5, 3.0, ((0, 8),)),
        "conv_out_weight": normal_values(streams_of[4], (TAPS, C, ZC), (TAPS * C // 4) ** -0.5, 0.109375, ((1, 8),)),
        "out_bias": normal_values(streams_of[5], (ZC,), 0.5, 3.0, (), jnp.float32),
        "patch_weight": normal_values(streams_of[6], (PATCH, HID), (PATCH // 4) ** -0.5, 1.5),
        "patch_bias": normal_values(streams_of[7], (HID,), 0.5, 3.0),
        "qkv_weight": normal_values(streams_of[8], (HID, HEADS * 3 * HD), HID ** -0.5, 0.109375, ((0, 64), (1, 8))),
        "qkv_bias": normal_values(streams_of[9], (HEADS * 3 * HD,), 0.5, 3.0, ((0, 8),)),
        "q_gain": jnp.clip(1.0 + 0.18 * jax.random.normal(streams_of[10], (HD,), jnp.float32), 0.099609375, 1.8984375).astype(jnp.bfloat16),
        "k_gain": jnp.clip(1.0 + 0.18 * jax.random.normal(streams_of[11], (HD,), jnp.float32), 0.099609375, 1.8984375).astype(jnp.bfloat16),
        "frame_pos": plant(jax.random.randint(streams_of[12], (FRAMES,), 0, 64), jax.random.fold_in(streams_of[12], 1), 0, 63).astype(jnp.int32),
        "row_pos": plant(jax.random.randint(streams_of[13], (TROWS,), 0, 128), jax.random.fold_in(streams_of[13], 1), 0, 127).astype(jnp.int32),
    }


norm_eps = 1e-06
latent_scale = 0.476986
rope_base = 256.0
time_dims = 16
row_dims = 56

def extend(block):
    return jnp.pad(block, ((2, 0), (1, 1), (1, 1), (0, 0)), mode='edge')

def convolve(padded, weight):
    frames = padded.shape[0] - 2
    rows = padded.shape[1] - 2
    cols = padded.shape[2] - 2
    total = jnp.zeros((frames * rows * cols, weight.shape[2]), jnp.float32)
    for shift_t in range(3):
        for shift_r in range(3):
            for shift_c in range(3):
                window = padded[shift_t:shift_t + frames, shift_r:shift_r + rows, shift_c:shift_c + cols]
                window = window.reshape(-1, padded.shape[3])
                total = total + jnp.dot(window, weight[9 * shift_t + 3 * shift_r + shift_c], preferred_element_type=jnp.float32)
    return total.reshape(frames, rows, cols, weight.shape[2])

def section_freqs(dims):
    return jnp.power(rope_base, -jnp.arange(0, dims, 2, dtype=jnp.float32) / dims)

def rope_angles(tpos, hpos, width):
    frames = tpos.shape[0]
    rows = hpos.shape[0]
    cols = jnp.arange(width, dtype=jnp.float32)
    part_t = tpos[:, None, None, None] * section_freqs(time_dims)
    part_h = hpos[None, :, None, None] * section_freqs(row_dims)
    part_w = cols[None, None, :, None] * section_freqs(row_dims)
    shape = (frames, rows, width)
    return jnp.concatenate([jnp.broadcast_to(part_t, shape + (time_dims // 2,)), jnp.broadcast_to(part_h, shape + (row_dims // 2,)), jnp.broadcast_to(part_w, shape + (row_dims // 2,))], axis=-1)

def rotate(vectors, angles):
    pairs = vectors.reshape(vectors.shape[:-1] + (vectors.shape[-1] // 2, 2))
    first = pairs[..., 0]
    second = pairs[..., 1]
    cosine = jnp.cos(angles)[..., None, :]
    sine = jnp.sin(angles)[..., None, :]
    turned = jnp.stack([first * cosine - second * sine, first * sine + second * cosine], axis=-1)
    return turned.reshape(vectors.shape)

def rms_scale(vectors, gain):
    return vectors * lax.rsqrt(lax.optimization_barrier(jnp.mean(vectors * vectors, axis=-1, keepdims=True)) + norm_eps) * gain.astype(jnp.float32)

def reference(clip_inputs, conv_in_weight, group_gain, group_bias, conv_out_weight, out_bias, patch_weight, patch_bias, qkv_weight, qkv_bias, q_gain, k_gain, frame_pos, row_pos):
    weight_in = conv_in_weight.reshape(TAPS, C, C)
    angles = rope_angles(frame_pos.astype(jnp.float32), row_pos.astype(jnp.float32), TCOLS)

    def one_clip(block):
        hidden = convolve(extend(block), weight_in)
        grouped = hidden.reshape(-1, GROUPS, C // GROUPS)
        mean = lax.optimization_barrier(jnp.mean(grouped, axis=(0, 2)))
        var = lax.optimization_barrier(jnp.mean(grouped * grouped, axis=(0, 2))) - mean * mean
        scaled = (grouped - mean[None, :, None]) * lax.rsqrt(var + norm_eps)[None, :, None]
        scaled = scaled.reshape(hidden.shape) * group_gain.astype(jnp.float32) + group_bias.astype(jnp.float32)
        normed = jax.nn.silu(scaled).astype(jnp.bfloat16)
        latent = (convolve(extend(normed), conv_out_weight) + out_bias) * latent_scale
        latent_bf = latent.astype(jnp.bfloat16)
        patches = latent_bf.reshape(FRAMES, TROWS, 2, TCOLS, 2, ZC).transpose(0, 1, 3, 2, 4, 5).reshape(-1, PATCH)
        embedded = (jnp.dot(patches, patch_weight, preferred_element_type=jnp.float32) + patch_bias.astype(jnp.float32)).astype(jnp.bfloat16)
        projected = jnp.dot(embedded, qkv_weight, preferred_element_type=jnp.float32) + qkv_bias.astype(jnp.float32)
        projected = projected.reshape(FRAMES, TROWS, TCOLS, HEADS, 3, HD)
        query = rotate(rms_scale(projected[..., 0, :], q_gain), angles)
        key = rotate(rms_scale(projected[..., 1, :], k_gain), angles)
        value = projected[..., 2, :]
        merged = (FRAMES, TROWS, TCOLS, HEADS * HD)
        return (latent.reshape(FRAMES, ROWS, COLS * ZC), query.reshape(merged).astype(jnp.bfloat16), key.reshape(merged).astype(jnp.bfloat16), value.reshape(merged).astype(jnp.bfloat16))
    latents, queries, keys, values = lax.map(one_clip, clip_inputs)
    return (latents, queries, keys, values)
```

```python
import math

import jax
import jax.numpy as jnp
from jax import lax
from jax.experimental import pallas as pl
from jax.experimental.pallas import tpu as pltpu
from jax.sharding import PartitionSpec as P

HD = 128
GROUPS = 32
TAPS = 27
N = 8

norm_eps = 1e-06
latent_scale = 0.476986
rope_base = 256.0
time_dims = 16
row_dims = 56

F32 = jnp.float32
BF16 = jnp.bfloat16
MESH = pl.DeviceIdType.MESH

SLOT_STEP = (0, -1, 1, -2, 2, -3, 3, -4)

NT = (((1,), (1,)), ((), ()))


def iota(shape, dim):
    return lax.broadcasted_iota(jnp.int32, shape, dim)


def chunk(ref, which):
    if which == 0:
        return ref.at[pl.ds(2, 2), pl.ds(1, 2)]
    if which == 1:
        return ref.at[pl.ds(0, 2), pl.ds(1, 2)]
    if which == 2:
        return ref.at[pl.ds(0, 4), pl.ds(0, 1)]
    return ref.at[pl.ds(0, 4), pl.ds(3, 1)]


def kernel(
    x_ref,
    wi_ref,
    gg_ref,
    gb_ref,
    wo_ref,
    ob_ref,
    pw_ref,
    pb_ref,
    qw_ref,
    qb_ref,
    qg_ref,
    kg_ref,
    fp_ref,
    rp_ref,
    lat_ref,
    q_ref,
    k_ref,
    v_ref,
    xe,
    wg,
    bt,
    ht,
    w2,
    place,
    wp,
    wr,
    wsum,
    wrh,
    wth,
    wf,
    wcc,
    st,
    str_t,
    str_h,
    outs,
    rz,
    ext,
    rh,
    pb,
    trig,
    zr_s,
    zr_r,
    zl_s,
    zl_r,
    ha_s,
    ha_r,
    wx_s,
    wx_r,
    yr_s,
    yr_r,
    yl_s,
    yl_r,
    co_s,
    co_r,
    wc_s,
    wc_r,
    ss_s,
    ss_r,
    rz_s,
    rz_r,
    rh_s,
    rh_r,
    pb_s,
    pb_r,
):
    z = lax.axis_index("dp")
    tm = lax.axis_index("tm")
    hh = lax.axis_index("height")
    core = lax.rem(tm, 2)
    y_lo = tm // 2
    x = hh // 2
    y_hi = lax.rem(hh, 2)
    y = y_hi * 4 + y_lo

    def at_y(where):
        return (z, lax.rem(where, 4) * 2 + core, x * 2 + where // 4)

    def remote(src, dst, send, recv, device):
        return pltpu.make_async_remote_copy(
            src_ref=src,
            dst_ref=dst,
            send_sem=send,
            recv_sem=recv,
            device_id=device,
            device_id_type=MESH,
        )

    z_up = (lax.rem(z + 1, N), tm, hh)
    z_down = (lax.rem(z + N - 1, N), tm, hh)
    y_up = at_y(lax.rem(y + 1, N))
    y_down = at_y(lax.rem(y + N - 1, N))
    other_core = (z, tm + 1 - 2 * core, hh)

    barrier = pltpu.get_barrier_semaphore()

    def greet(k, _):
        for device in (
            (lax.rem(z + k, N), tm, hh),
            (z, lax.rem(tm + k, N), hh),
            (z, tm, lax.rem(hh + k, N)),
        ):
            pl.semaphore_signal(barrier, inc=1, device_id=device, device_id_type=MESH)
        return 0

    lax.fori_loop(1, N, greet, 0)
    for dt in (1, N - 1):
        for dh in (1, N - 1):
            device = (z, lax.rem(tm + dt, N), lax.rem(hh + dh, N))
            pl.semaphore_signal(barrier, inc=1, device_id=device, device_id_type=MESH)
    for device in (y_up, y_down):
        pl.semaphore_signal(barrier, inc=1, device_id=device, device_id_type=MESH)

    eye = (iota((64, 64), 0) == iota((64, 64), 1)).astype(BF16)
    shard = lax.dot_general(eye, wi_ref[...], NT, preferred_element_type=F32)
    wg[y, core, x] = jnp.zeros((64, 256), BF16)
    wg[y, core, x, :, pl.ds(0, 216)] = shard.astype(BF16)

    d = tm * N + hh
    tile = jnp.minimum(48 * d // 128, 22)
    shift = 48 * d - 128 * tile
    window = pl.ds(pl.multiple_of(tile * 128, 128), 256)
    embed = jnp.concatenate(
        [pw_ref[:, window].astype(F32), jnp.broadcast_to(pb_ref[:, window].astype(F32), (8, 256))],
        axis=0,
    )
    embed = pltpu.roll(embed, lax.rem(256 - shift, 256), 1)[:, :48].astype(BF16)
    part = jnp.dot(embed, qw_ref[...], preferred_element_type=F32)
    for row in range(9):
        for lane in range(6):
            wp[row * 6 + lane] = part[8 * row : 8 * row + 8, 128 * lane : 128 * lane + 128]
    wp[pl.ds(54, 10)] = jnp.zeros((10, 8, 128), F32)

    pl.semaphore_wait(barrier, 27)

    def z_right(step, part):
        src = chunk(xe.at[SLOT_STEP.index(-step + 1) if step > 1 else 0], part)
        if step == 1 and part == 0:
            src = x_ref
        return remote(
            src,
            chunk(xe.at[SLOT_STEP.index(-step)], part),
            zr_s.at[step - 1, part],
            zr_r.at[step - 1, part],
            z_up,
        )

    def z_left(step, part):
        src = chunk(xe.at[SLOT_STEP.index(step - 1)], part)
        if step == 1 and part == 0:
            src = x_ref
        return remote(
            src,
            chunk(xe.at[SLOT_STEP.index(step)], part),
            zl_s.at[step - 1, part],
            zl_r.at[step - 1, part],
            z_down,
        )

    own = xe.at[0]
    has_next = tm < N - 1
    has_last = tm > 0
    has_up = hh < N - 1
    has_down = hh > 0
    next_tm = lax.rem(tm + 1, N)
    up_h = lax.rem(hh + 1, N)
    down_h = lax.rem(hh + N - 1, N)
    row_0 = x_ref.at[:, pl.ds(0, 1)]
    row_1 = x_ref.at[:, pl.ds(1, 1)]
    halos = (
        (x_ref, own.at[pl.ds(0, 2), pl.ds(1, 2)], (z, next_tm, hh), has_next, has_last),
        (row_0, own.at[pl.ds(2, 2), pl.ds(3, 1)], (z, tm, down_h), has_down, has_up),
        (row_1, own.at[pl.ds(2, 2), pl.ds(0, 1)], (z, tm, up_h), has_up, has_down),
        (
            row_0,
            own.at[pl.ds(0, 2), pl.ds(3, 1)],
            (z, next_tm, down_h),
            has_next & has_down,
            has_last & has_up,
        ),
        (
            row_1,
            own.at[pl.ds(0, 2), pl.ds(0, 1)],
            (z, next_tm, up_h),
            has_next & has_up,
            has_last & has_down,
        ),
    )

    def halo_copy(i):
        src, dst, device, _, _ = halos[i]
        return remote(src, dst, ha_s.at[i], ha_r.at[i], device)

    z_right(1, 0).start()
    z_left(1, 0).start()
    for i in range(5):
        pl.when(halos[i][3])(lambda i=i: halo_copy(i).start())

    def x_copy(k):
        return remote(
            wg.at[y, core, x],
            wg.at[y, core, x],
            wx_s.at[k],
            wx_r.at[k],
            (z, tm, lax.rem(hh + 2 * k, N)),
        )

    def x_wait(k):
        from_x = lax.rem(x + 4 - k, 4)
        remote(
            wg.at[y, core, x],
            wg.at[y, core, from_x],
            wx_s.at[k],
            wx_r.at[k],
            (z, tm, lax.rem(hh + 2 * k, N)),
        ).wait_recv()

    for k in range(1, 4):
        x_copy(k).start()

    def fold_1(k):
        to = lax.rem(tm + k, N)
        return remote(
            wp.at[pl.ds(8 * to, 8)], wr.at[k], wc_s.at[0, k], wc_r.at[0, k], (z, to, hh)
        )

    def fold_2(k):
        to = lax.rem(hh + k, N)
        return remote(wsum.at[to], wrh.at[k], wc_s.at[1, k], wc_r.at[1, k], (z, tm, to))

    def fold_3(k, source):
        to = lax.rem(hh + k, N)
        return remote(
            wth.at[hh], wth.at[source], wc_s.at[2, k], wc_r.at[2, k], (z, tm, to)
        )

    def fold_4(k, source):
        to = lax.rem(tm + k, N)
        return remote(
            wf.at[tm], wf.at[source], wc_s.at[3, k], wc_r.at[3, k], (z, to, hh)
        )

    def each(fn):
        def body(k, _):
            fn(k)
            return 0

        lax.fori_loop(1, N, body, 0)

    each(lambda k: fold_1(k).start())

    xe[0, 2:4, 1:3] = x_ref[...]

    eye16 = (iota((16, 16), 0) == iota((16, 16), 1)).astype(BF16)
    for ij in range(9):
        w2[16 * ij : 16 * ij + 16] = jnp.concatenate(
            [
                lax.dot_general(eye16, wo_ref[3 * ij + l], NT, preferred_element_type=F32)
                for l in range(3)
            ],
            axis=1,
        ).astype(BF16)

    for k in range(1, 4):
        x_wait(k)

    def y_right(step):
        from_y = lax.rem(y + N - step + 1, N)
        return remote(
            wg.at[from_y, core], wg.at[from_y, core], yr_s.at[step - 1], yr_r.at[step - 1], y_up
        )

    def y_right_wait(step):
        from_y = lax.rem(y + N - step, N)
        remote(
            wg.at[from_y, core], wg.at[from_y, core], yr_s.at[step - 1], yr_r.at[step - 1], y_up
        ).wait_recv()

    def y_left(step):
        from_y = lax.rem(y + step - 1, N)
        return remote(
            wg.at[from_y, core], wg.at[from_y, core], yl_s.at[step - 1], yl_r.at[step - 1], y_down
        )

    def y_left_wait(step):
        from_y = lax.rem(y + step, N)
        remote(
            wg.at[from_y, core], wg.at[from_y, core], yl_s.at[step - 1], yl_r.at[step - 1], y_down
        ).wait_recv()

    def core_copy(slot):
        from_y = lax.rem(y + N + SLOT_STEP[slot], N)
        return remote(
            wg.at[from_y, core], wg.at[from_y, core], co_s.at[slot], co_r.at[slot], other_core
        )

    def core_wait(slot):
        from_y = lax.rem(y + N + SLOT_STEP[slot], N)
        other = 1 - core
        remote(
            wg.at[from_y, other], wg.at[from_y, other], co_s.at[slot], co_r.at[slot], other_core
        ).wait_recv()

    y_right(1).start()
    y_left(1).start()
    core_copy(0).start()

    def halo_wait(i, fill):
        pl.when(halos[i][4])(lambda: halo_copy(i).wait_recv())
        if fill is not None:
            pl.when(jnp.logical_not(halos[i][4]))(fill)

    def first_frames():
        first = x_ref[0:1]
        xe[0, 0:1, 1:3] = first
        xe[0, 1:2, 1:3] = first

    halo_wait(0, first_frames)
    z_right(1, 1).start()
    z_left(1, 1).start()
    for i in range(1, 5):
        halo_wait(i, None)

    def first_corner(row):
        def fill():
            edge = xe[0, 2:3, row : row + 1]
            xe[0, 0:1, row : row + 1] = edge
            xe[0, 1:2, row : row + 1] = edge

        return fill

    @pl.when(jnp.logical_not(has_last) & has_down)
    def _():
        first_corner(0)()

    @pl.when(jnp.logical_not(has_last) & has_up)
    def _():
        first_corner(3)()

    @pl.when(jnp.logical_not(has_down))
    def _():
        xe[0, :, 0:1] = xe[0, :, 1:2]

    @pl.when(jnp.logical_not(has_up))
    def _():
        xe[0, :, 3:4] = xe[0, :, 2:3]

    for part in (2, 3):
        z_right(1, part).start()
        z_left(1, part).start()

    def ring_step(step):
        for part in range(4):
            z_right(step, part).wait_recv()
            z_right(step + 1, part).start()
            z_left(step, part).wait_recv()
            if step < 3:
                z_left(step + 1, part).start()

    def weight_step(step):
        y_right_wait(step)
        if step < 4:
            y_right(step + 1).start()
        core_copy(2 * step - 1).start()
        if step < 4:
            y_left_wait(step)
            if step < 3:
                y_left(step + 1).start()
            core_copy(2 * step).start()

    ring_step(1)
    weight_step(1)

    each(lambda k: fold_1(k).wait_recv())
    total = wp[pl.ds(8 * tm, 8)]
    for k in range(1, N):
        total = total + wr[k]
    wsum[...] = total
    each(lambda k: fold_2(k).start())

    ring_step(2)
    weight_step(2)

    each(lambda k: fold_2(k).wait_recv())
    tile_sum = wsum[hh]
    for k in range(1, N):
        tile_sum = tile_sum + wrh[k]
    wth[hh] = tile_sum
    each(lambda k: fold_3(k, hh).start())

    ring_step(3)
    weight_step(3)

    each(lambda k: fold_3(k, lax.rem(hh + N - k, N)).wait_recv())
    wf[tm] = wth[...]
    each(lambda k: fold_4(k, tm).start())

    lane = iota((128, 512), 1)
    row = iota((128, 512), 0)
    s_at = (lane >> 6) & 3
    q_at = (lane >> 4) & 3
    f_at = (row >> 5) & 1
    r_at = (row >> 4) & 1
    in_frame = (s_at == f_at + 2) | ((tm == 0) & (s_at < 2) & (f_at == 0))
    in_row = (
        (q_at == r_at + 1)
        | ((hh == 0) & (q_at == 0) & (r_at == 0))
        | ((hh == N - 1) & (q_at == 3) & (r_at == 1))
    )
    same = ((lane & 15) == (row & 15)) & ((lane >> 8) == (row >> 6))
    place[...] = jnp.where(in_frame & in_row & same, 1.0, 0.0).astype(BF16)

    entry = iota((16, 128), 1) >> 1
    token = iota((16, 128), 0)
    is_frame = entry < 8
    is_row = entry < 36
    start = jnp.where(is_frame, 0, jnp.where(is_row, 8, 36))
    width = jnp.where(is_frame, float(time_dims), float(row_dims))
    power = 2.0 * (entry - start).astype(F32) / width
    freq = jnp.exp(power * (-math.log(rope_base)))
    frame_at = jnp.where(token < 8, fp_ref[0].astype(F32), fp_ref[1].astype(F32))
    spot = jnp.where(
        is_frame,
        frame_at,
        jnp.where(is_row, rp_ref[0].astype(F32), (token & 7).astype(F32)),
    )
    angle = spot * freq
    trig[0] = jnp.cos(angle)
    odd = (iota((16, 128), 1) & 1) == 1
    sine = jnp.sin(angle)
    trig[1] = jnp.where(odd, sine, -sine)

    weight_step(4)
    for slot in range(N):
        core_wait(slot)

    def shard_of(index):
        t, h = index // N, index % N
        return wg[(h % 2) * 4 + t // 2, t % 2, h // 2]

    for tile in range(4 * TAPS):
        source, first = (128 * tile) // 216, (128 * tile) % 216
        count = min(128, 216 - first)
        value = shard_of(source)[:, first : first + count]
        if count < 128:
            value = jnp.concatenate([value, shard_of(source + 1)[:, : 128 - count]], axis=1)
        tap = tile // 4
        ij, l = tap // 3, tap % 3
        at = 128 * (tile % 4)
        bt[ij, 64 * l : 64 * l + 64, at : at + 128] = value

    col = iota((64, 128), 1) & 15

    def conv_pair(pair):
        total = jnp.zeros((192, 128), F32)
        for ij in range(9):
            i, j = ij // 3, ij % 3
            block = xe[2 * pair : 2 * pair + 2, i : i + 2, j : j + 2].reshape(128, 512)
            total = total + lax.dot_general(bt[ij], block, NT, preferred_element_type=F32)
        left, mid, right = total[:64], total[64:128], total[128:]
        left = jnp.where(col == 0, left, pltpu.roll(left, 1, 1))
        right = jnp.where(col == 15, right, pltpu.roll(right, 127, 1))
        ht[pair] = left + mid + right

    for pair in range(3):
        conv_pair(pair)
    for part in range(4):
        z_right(4, part).wait_recv()
    conv_pair(3)

    stat_lane = iota((8, 128), 1)
    compact = jnp.zeros((8, 128), F32)
    for pair in range(4):
        value = ht[pair]
        sums = jnp.sum(value.reshape(4, 16, 128), axis=1)
        squares = jnp.sum((value * value).reshape(4, 16, 128), axis=1)
        both = jnp.concatenate([sums, squares], axis=0)
        low = jnp.sum(jnp.where(stat_lane < 64, both, 0.0), axis=1, keepdims=True)
        high = jnp.sum(jnp.where(stat_lane >= 64, both, 0.0), axis=1, keepdims=True)
        compact = jnp.where(stat_lane == pair, low, compact)
        compact = jnp.where(stat_lane == 64 + pair, high, compact)
    st[0] = compact

    def stat_1(k):
        to = lax.rem(tm + k, N)
        return remote(st.at[0], str_t.at[k], ss_s.at[0, k], ss_r.at[0, k], (z, to, hh))

    def stat_2(k):
        to = lax.rem(hh + k, N)
        return remote(st.at[1], str_h.at[k], ss_s.at[1, k], ss_r.at[1, k], (z, tm, to))

    each(lambda k: stat_1(k).start())

    each(lambda k: fold_4(k, lax.rem(tm + N - k, N)).wait_recv())

    each(lambda k: stat_1(k).wait_recv())
    for k in range(1, N):
        compact = compact + str_t[k]
    st[1] = compact
    each(lambda k: stat_2(k).start())

    for lane_tile in range(6):
        for pair in range(4):
            tiles = [12 * pair + lane_tile, 12 * pair + 6 + lane_tile]
            value = jnp.concatenate([wf[t // 8, t % 8] for t in tiles], axis=0)
            high = value.astype(BF16)
            low = (value - high.astype(F32)).astype(BF16)
            at = slice(128 * lane_tile, 128 * lane_tile + 128)
            wcc[16 * pair : 16 * pair + 16, at] = high
            wcc[64 + 16 * pair : 64 + 16 * pair + 16, at] = low

    diag = iota((64, 64), 0) == iota((64, 64), 1)
    gain = jnp.sum(jnp.where(diag, gg_ref[...].astype(F32), 0.0), axis=1, keepdims=True)
    bias = jnp.sum(jnp.where(diag, gb_ref[...].astype(F32), 0.0), axis=1, keepdims=True)
    diag = iota((16, 16), 0) == iota((16, 16), 1)
    out_bias = jnp.sum(jnp.where(diag, ob_ref[...], 0.0), axis=1, keepdims=True)

    each(lambda k: stat_2(k).wait_recv())
    for k in range(1, N):
        compact = compact + str_h[k]
    count = float(16 * 16 * 16 * 16)
    average = compact / count
    mean = average
    var = pltpu.roll(average, 4, 0) - mean * mean
    inv = lax.rsqrt(var + norm_eps)

    wide = iota((16, 512), 1)
    t_at = (wide >> 6) & 3
    u_at = (wide >> 4) & 3
    lane_128 = iota((8, 128), 1)

    def spread(value, pair):
        lanes = jnp.where(
            lane_128 < 64,
            jnp.broadcast_to(value[:, pair : pair + 1], (8, 128)),
            jnp.broadcast_to(value[:, 64 + pair : 65 + pair], (8, 128)),
        )
        return jnp.concatenate(
            [jnp.broadcast_to(lanes[g : g + 1], (16, 128)) for g in range(4)], axis=0
        )

    def rz_copy(slot):
        to = lax.rem(z + N + SLOT_STEP[slot], N)
        return remote(outs.at[slot], rz.at[slot], rz_s.at[slot], rz_r.at[slot], (to, tm, hh))

    for pair in (3, 2, 1, 0):
        scale = spread(inv, pair) * gain
        offset = bias - spread(mean, pair) * scale
        value = ht[pair] * scale + offset
        value = value / (1.0 + jnp.exp(-value))
        left = jnp.where(col == 0, value, pltpu.roll(value, 1, 1))
        right = jnp.where(col == 15, value, pltpu.roll(value, 127, 1))
        stacked = jnp.concatenate([left, value, right], axis=0).astype(BF16)
        spots = jnp.dot(stacked, place[...], preferred_element_type=F32).astype(BF16)
        taps = jnp.dot(w2[...], spots, preferred_element_type=F32)
        total = jnp.zeros((16, 512), F32)
        for ij in range(9):
            i, j = ij // 3, ij % 3
            move = (16 * (1 - j) - 64 * i) % 512
            moved = taps[16 * ij : 16 * ij + 16]
            if move:
                moved = pltpu.roll(moved, move, 1)
            valid = t_at <= 3 - i
            if j == 0:
                valid = valid & (u_at >= 1)
            if j == 2:
                valid = valid & (u_at <= 2)
            total = total + jnp.where(valid, moved, 0.0)
        outs[2 * pair] = total[:, :256]
        outs[2 * pair + 1] = total[:, 256:]
        for slot in (2 * pair + 1, 2 * pair):
            if slot:
                rz_copy(slot).start()

    for i in range(5):

        @pl.when(jnp.logical_not(halos[i][4]))
        def _(i=i):
            rh[i] = jnp.zeros((16, 128), F32)

    total = outs[0]
    for slot in range(1, N):
        rz_copy(slot).wait_recv()
        total = total + rz[slot]
    ext[0] = total[:, :128]
    ext[1] = total[:, 128:]

    def rh_copy(i):
        return remote(
            ext.at[1 if i in (0, 3, 4) else 0],
            rh.at[i],
            rh_s.at[i],
            rh_r.at[i],
            halos[i][2],
        )

    for i in range(5):
        pl.when(halos[i][3])(lambda i=i: rh_copy(i).start())
    for i in range(5):
        pl.when(halos[i][4])(lambda i=i: rh_copy(i).wait_recv())

    narrow = iota((16, 128), 1)
    u_at = (narrow >> 4) & 3
    inside = (u_at == 1) | (u_at == 2)
    latent = jnp.where(inside, total[:, :128] + rh[0], 0.0)
    latent = latent + jnp.where(u_at == 2, pltpu.roll(rh[1] + rh[3], 32, 1), 0.0)
    latent = latent + jnp.where(u_at == 1, pltpu.roll(rh[2] + rh[4], 96, 1), 0.0)
    latent = (latent + out_bias) * latent_scale

    lane = iota((128, 128), 1)
    group = (iota((128, 128), 0) >> 4) & 3
    keep = (((lane >> 4) & 3) == (group >> 1) + 1) & ((lane & 1) == (group & 1))
    rounded = latent.astype(BF16).astype(F32)
    many = jnp.where(keep, jnp.concatenate([rounded] * 8, axis=0), 0.0).astype(BF16)
    lane = iota((16, 128), 1)
    row = iota((16, 128), 0)
    pick = ((lane >> 6) == (row >> 3)) & (((lane & 15) >> 1) == (row & 7))
    pick = jnp.where(pick, 1.0, 0.0).astype(BF16)
    pb[z] = lax.dot_general(pick, many, NT, preferred_element_type=F32).astype(BF16)

    def pb_copy(k, source):
        return remote(
            pb.at[z],
            pb.at[source],
            pb_s.at[k],
            pb_r.at[k],
            (lax.rem(z + k, N), tm, hh),
        )

    each(lambda k: pb_copy(k, z).start())

    lane = iota((256, 128), 1)
    row = iota((256, 128), 0)
    many = jnp.where((lane & 15) == (row >> 4), jnp.concatenate([latent] * 16, axis=0), 0.0)
    lane = iota((8, 128), 1)
    row = iota((8, 128), 0)
    pick = ((lane >> 6) == (row >> 1)) & (((lane >> 4) & 3) == (row & 1) + 1)
    pick = jnp.where(pick, 1.0, 0.0)
    lines = lax.dot_general(
        pick, many, NT, preferred_element_type=F32, precision=lax.Precision.HIGHEST
    )
    lat_ref[...] = lines[:4]

    folded_bias = jnp.concatenate(
        [wf[6 + lane_tile // 8, lane_tile % 8][0:1] for lane_tile in range(6)], axis=1
    ) + qb_ref[...].astype(F32)
    cosine = jnp.concatenate([trig[0]] * 8, axis=0)
    sine = jnp.concatenate([trig[1]] * 8, axis=0)
    odd = (iota((128, 128), 1) & 1) == 1

    each(lambda k: pb_copy(k, lax.rem(z + N - k, N)).wait_recv())

    projected = jnp.dot(pb[...].reshape(128, 128), wcc[...], preferred_element_type=F32)
    projected = projected + folded_bias

    def turned(value, gain):
        mean_square = jnp.mean(value * value, axis=1, keepdims=True)
        value = value * lax.rsqrt(mean_square + norm_eps) * gain
        swapped = jnp.where(odd, pltpu.roll(value, 1, 1), pltpu.roll(value, 127, 1))
        return (value * cosine + swapped * sine).astype(BF16)

    q_gain = qg_ref[...].astype(F32)
    k_gain = kg_ref[...].astype(F32)
    for head in range(2):
        at = slice(HD * head, HD * head + HD)
        base = 3 * HD * head
        q_ref[:, at] = turned(projected[:, base : base + HD], q_gain)
        k_ref[:, at] = turned(projected[:, base + HD : base + 2 * HD], k_gain)
        v_ref[:, at] = projected[:, base + 2 * HD : base + 3 * HD].astype(BF16)

    for step in range(1, 5):
        for part in range(4):
            z_right(step, part).wait_send()
            if step < 4:
                z_left(step, part).wait_send()
        y_right(step).wait_send()
        if step < 4:
            y_left(step).wait_send()
    for i in range(5):
        pl.when(halos[i][3])(lambda i=i: halo_copy(i).wait_send())
        pl.when(halos[i][3])(lambda i=i: rh_copy(i).wait_send())
    for k in range(1, 4):
        x_copy(k).wait_send()
    for slot in range(N):
        core_copy(slot).wait_send()
        if slot:
            rz_copy(slot).wait_send()

    def sent(k):
        fold_1(k).wait_send()
        fold_2(k).wait_send()
        fold_3(k, hh).wait_send()
        fold_4(k, tm).wait_send()
        stat_1(k).wait_send()
        stat_2(k).wait_send()
        pb_copy(k, z).wait_send()

    each(sent)


def shards(
    clip_inputs,
    conv_in_weight,
    group_gain,
    group_bias,
    conv_out_weight,
    out_bias,
    patch_weight,
    patch_bias,
    qkv_weight,
    qkv_bias,
    q_gain,
    k_gain,
    frame_pos,
    row_pos,
):
    vmem = pl.BlockSpec(memory_space=pltpu.VMEM)
    smem = pl.BlockSpec(memory_space=pltpu.SMEM)
    dma = pltpu.SemaphoreType.DMA
    latents, queries, keys, values = pl.pallas_call(
        kernel,
        out_shape=(
            jax.ShapeDtypeStruct((4, 256), F32),
            jax.ShapeDtypeStruct((128, 256), BF16),
            jax.ShapeDtypeStruct((128, 256), BF16),
            jax.ShapeDtypeStruct((128, 256), BF16),
        ),
        in_specs=[vmem] * 12 + [smem] * 2,
        out_specs=(vmem,) * 4,
        scratch_shapes=[
            pltpu.VMEM((N, 4, 4, 16, 512), BF16),
            pltpu.VMEM((N, 2, 4, 64, 256), BF16),
            pltpu.VMEM((9, 192, 512), BF16),
            pltpu.VMEM((4, 64, 128), F32),
            pltpu.VMEM((144, 192), BF16),
            pltpu.VMEM((128, 512), BF16),
            pltpu.VMEM((64, 8, 128), F32),
            pltpu.VMEM((N, 8, 8, 128), F32),
            pltpu.VMEM((8, 8, 128), F32),
            pltpu.VMEM((N, 8, 128), F32),
            pltpu.VMEM((N, 8, 128), F32),
            pltpu.VMEM((N, 8, 8, 128), F32),
            pltpu.VMEM((128, 768), BF16),
            pltpu.VMEM((2, 8, 128), F32),
            pltpu.VMEM((N, 8, 128), F32),
            pltpu.VMEM((N, 8, 128), F32),
            pltpu.VMEM((N, 16, 256), F32),
            pltpu.VMEM((N, 16, 256), F32),
            pltpu.VMEM((2, 16, 128), F32),
            pltpu.VMEM((5, 16, 128), F32),
            pltpu.VMEM((N, 16, 128), BF16),
            pltpu.VMEM((2, 16, 128), F32),
            dma((4, 4)),
            dma((4, 4)),
            dma((3, 4)),
            dma((3, 4)),
            dma((5,)),
            dma((5,)),
            dma((4,)),
            dma((4,)),
            dma((4,)),
            dma((4,)),
            dma((3,)),
            dma((3,)),
            dma((N,)),
            dma((N,)),
            dma((4, N)),
            dma((4, N)),
            dma((2, N)),
            dma((2, N)),
            dma((N,)),
            dma((N,)),
            dma((5,)),
            dma((5,)),
            dma((N,)),
            dma((N,)),
        ],
        compiler_params=pltpu.CompilerParams(
            collective_id=0, has_side_effects=True, vmem_limit_bytes=48 * 2**20
        ),
    )(
        clip_inputs[0],
        conv_in_weight,
        group_gain[None],
        group_bias[None],
        conv_out_weight,
        out_bias[None],
        patch_weight,
        patch_bias[None],
        qkv_weight,
        qkv_bias[None],
        q_gain[None],
        k_gain[None],
        frame_pos,
        row_pos,
    )
    merged = (N, 2, 1, 8, 2 * HD)
    return (
        latents.reshape(1, 2, 2, 256),
        queries.reshape(merged),
        keys.reshape(merged),
        values.reshape(merged),
    )


def solution(mesh):
    placed = (
        P("dp", "tm", "height", None, None),
        P(("tm", "height"), "dp"),
        P("dp"),
        P("dp"),
        P(None, "dp", None),
        P(),
        P(),
        P(),
        P(("tm", "height"), "dp"),
        P("dp"),
        P(),
        P(),
        P("tm"),
        P("height"),
    )
    return jax.shard_map(
        shards,
        mesh=mesh,
        in_specs=placed,
        out_specs=(
            P("dp", "tm", "height", None),
            P(None, "tm", "height", None, "dp"),
            P(None, "tm", "height", None, "dp"),
            P(None, "tm", "height", None, "dp"),
        ),
        check_vma=False,
    )
```

```python
import math

import jax
import jax.numpy as jnp
from jax import lax
from jax.experimental import pallas as pl
from jax.experimental.pallas import tpu as pltpu
from jax.sharding import PartitionSpec as P

HD = 128
GROUPS = 32
TAPS = 27
N = 8

norm_eps = 1e-06
latent_scale = 0.476986
rope_base = 256.0
time_dims = 16
row_dims = 56

F32 = jnp.float32
BF16 = jnp.bfloat16
MESH = pl.DeviceIdType.MESH

SLOT_STEP = (0, -1, 1, -2, 2, -3, 3, -4)

ROW = (2, 0, 1, 3)

NT = (((1,), (1,)), ((), ()))


def iota(shape, dim):
    return lax.broadcasted_iota(jnp.int32, shape, dim)


def part_of(ref, which):
    frames, rows = ((2, 0), (0, 0), (2, 2), (0, 2))[which]
    return ref.at[pl.ds(frames, 2), pl.ds(rows, 2)]


def kernel(
    x_ref,
    wi_ref,
    gg_ref,
    gb_ref,
    wo_ref,
    ob_ref,
    pw_ref,
    pb_ref,
    qw_ref,
    qb_ref,
    qg_ref,
    kg_ref,
    fp_ref,
    rp_ref,
    lat_ref,
    pat_ref,
    wcc_ref,
    bias_ref,
    trig_ref,
    xe,
    wi,
    gg,
    gb,
    wo,
    ob,
    pw,
    pbias,
    qw,
    qb,
    qg,
    kg,
    wg,
    bt,
    ht,
    w2,
    place,
    wp,
    wr,
    wsum,
    wrh,
    wth,
    wf,
    st,
    outs,
    rz,
    ext,
    rh,
    pb,
    in_sem,
    zr_s,
    zr_r,
    zl_s,
    zl_r,
    ha_s,
    ha_r,
    cc_s,
    cc_r,
    wy_s,
    wy_r,
    wx_s,
    wx_r,
    co_s,
    co_r,
    wc_s,
    wc_r,
    ss_s,
    ss_r,
    rz_s,
    rz_r,
    rh_s,
    rh_r,
    pb_s,
    pb_r,
):
    z = lax.axis_index("dp")
    tm = lax.axis_index("tm")
    hh = lax.axis_index("height")
    core = lax.rem(tm, 2)
    y_lo = tm // 2
    x = hh // 2
    y_hi = lax.rem(hh, 2)
    y = y_hi * 4 + y_lo

    def at_y(where):
        return (z, lax.rem(where, 4) * 2 + core, x * 2 + where // 4)

    def remote(src, dst, send, recv, device):
        return pltpu.make_async_remote_copy(
            src_ref=src,
            dst_ref=dst,
            send_sem=send,
            recv_sem=recv,
            device_id=device,
            device_id_type=MESH,
        )

    sent = []

    def go(copy):
        copy.start()
        sent.append(copy.wait_send)

    def go_if(condition, make):
        pl.when(condition)(lambda: make().start())
        sent.append(lambda: pl.when(condition)(lambda: make().wait_send()))

    def each(fn, end=N):
        def body(k, _):
            fn(k)
            return 0

        lax.fori_loop(1, end, body, 0)

    def go_each(make, end=N):
        each(lambda k: make(k).start(), end)
        sent.append(lambda: each(lambda k: make(k).wait_send(), end))

    def finish():
        for wait in sent:
            wait()

    z_up = (lax.rem(z + 1, N), tm, hh)
    z_down = (lax.rem(z + N - 1, N), tm, hh)
    other_core = (z, tm + 1 - 2 * core, hh)
    first_core = core == 0
    last_core = core == 1

    barrier = pltpu.get_barrier_semaphore()

    def greet(device):
        pl.semaphore_signal(barrier, inc=1, device_id=device, device_id_type=MESH)

    def in_plane(k):
        return (z, lax.rem(tm + k // N, N), lax.rem(hh + lax.rem(k, N), N))

    each(lambda k: greet((lax.rem(z + k, N), tm, hh)))
    each(lambda k: greet(in_plane(k)), N * N)

    d = tm * N + hh
    tile = jnp.minimum(48 * d // 128, 22)
    shift = 48 * d - 128 * tile
    window = pl.ds(pl.multiple_of(tile * 128, 128), 256)
    own = xe.at[0]
    staged = [
        (wi_ref, wi),
        (x_ref, part_of(own, 0)),
        (pw_ref.at[:, window], pw),
        (pb_ref, pbias),
        (qw_ref, qw),
        (wo_ref, wo),
        (gg_ref, gg),
        (gb_ref, gb),
        (ob_ref, ob),
        (qb_ref, qb),
        (qg_ref, qg),
        (kg_ref, kg),
    ]
    staged = [
        pltpu.make_async_copy(src, dst, in_sem.at[i]) for i, (src, dst) in enumerate(staged)
    ]
    for copy in staged:
        copy.start()

    wg[y, core, x] = jnp.zeros((64, 256), BF16)
    staged[0].wait()
    wg[y, core, x, :, pl.ds(0, 216)] = wi[...]
    staged[1].wait()

    pl.semaphore_wait(barrier, N - 1 + N * N - 1)

    def z_right(step, part):
        return remote(
            part_of(xe.at[SLOT_STEP.index(1 - step)], part),
            part_of(xe.at[SLOT_STEP.index(-step)], part),
            zr_s.at[step - 1, part],
            zr_r.at[step - 1, part],
            z_up,
        )

    def z_left(step, part):
        return remote(
            part_of(xe.at[SLOT_STEP.index(step - 1)], part),
            part_of(xe.at[SLOT_STEP.index(step)], part),
            zl_s.at[step - 1, part],
            zl_r.at[step - 1, part],
            z_down,
        )

    def z_first(part):
        if part in (0, 2):
            go(z_right(1, part))
            go(z_left(1, part))
        else:
            go_if(first_core, lambda: z_right(1, part))
            go_if(first_core, lambda: z_left(1, part))

    has_next = tm < N - 1
    has_last = tm > 0
    has_up = hh < N - 1
    has_down = hh > 0
    next_tm = lax.rem(tm + 1, N)
    up_h = lax.rem(hh + 1, N)
    down_h = lax.rem(hh + N - 1, N)
    row_0 = own.at[pl.ds(2, 2), pl.ds(0, 1)]
    row_1 = own.at[pl.ds(2, 2), pl.ds(1, 1)]
    halos = (
        (part_of(own, 0), part_of(own, 1), (z, next_tm, hh), has_next, has_last),
        (row_0, own.at[pl.ds(2, 2), pl.ds(3, 1)], (z, tm, down_h), has_down, has_up),
        (row_1, own.at[pl.ds(2, 2), pl.ds(2, 1)], (z, tm, up_h), has_up, has_down),
        (
            row_0,
            own.at[pl.ds(0, 2), pl.ds(3, 1)],
            (z, next_tm, down_h),
            last_core & has_next & has_down,
            first_core & has_last & has_up,
        ),
        (
            row_1,
            own.at[pl.ds(0, 2), pl.ds(2, 1)],
            (z, next_tm, up_h),
            last_core & has_next & has_up,
            first_core & has_last & has_down,
        ),
    )

    def halo_copy(i):
        src, dst, device, _, _ = halos[i]
        return remote(src, dst, ha_s.at[i], ha_r.at[i], device)

    def halo_wait(i):
        pl.when(halos[i][4])(lambda: halo_copy(i).wait_recv())

    for i in (3, 4, 1, 2, 0):
        go_if(halos[i][3], lambda i=i: halo_copy(i))
    z_first(0)

    def y_copy(k, source):
        return remote(
            wg.at[y, core, x],
            wg.at[source, core, x],
            wy_s.at[k],
            wy_r.at[k],
            at_y(lax.rem(y + k, N)),
        )

    def x_copy(k, i, source):
        line = lax.rem(y + N - k, N)
        return remote(
            wg.at[line, core, x],
            wg.at[line, core, source],
            wx_s.at[k, i],
            wx_r.at[k, i],
            (z, tm, lax.rem(hh + 2 * i, N)),
        )

    def core_copy(k, source):
        line = lax.rem(y + N - k, N)
        return remote(
            wg.at[line, core], wg.at[line, source], co_s.at[k], co_r.at[k], other_core
        )

    y_order = (1, 7, 2, 6, 3, 5, 4)
    for k in y_order:
        go(y_copy(k, y))
    for i in (1, 3, 2):
        go(x_copy(0, i, x))

    for copy in staged[2:5]:
        copy.wait()
    bias_rows = pbias[...].astype(F32)
    bias_tile = iota((24, 128), 0)
    bias_row = jnp.concatenate(
        [
            jnp.sum(jnp.where(bias_tile == tile + i, bias_rows, 0.0), axis=0, keepdims=True)
            for i in range(2)
        ],
        axis=1,
    )
    embed = jnp.concatenate([pw[...].astype(F32), jnp.broadcast_to(bias_row, (8, 256))], axis=0)
    embed = pltpu.roll(embed, lax.rem(256 - shift, 256), 1)[:, :48].astype(BF16)
    part = jnp.dot(embed, qw[...], preferred_element_type=F32)
    for row in range(9):
        for lane in range(6):
            wp[row * 6 + lane] = part[8 * row : 8 * row + 8, 128 * lane : 128 * lane + 128]
    wp[pl.ds(54, 10)] = jnp.zeros((10, 8, 128), F32)

    def fold_1(k):
        to = lax.rem(tm + k, N)
        return remote(
            wp.at[pl.ds(8 * to, 8)], wr.at[k], wc_s.at[0, k], wc_r.at[0, k], (z, to, hh)
        )

    def fold_2(k):
        to = lax.rem(hh + k, N)
        return remote(wsum.at[to], wrh.at[k], wc_s.at[1, k], wc_r.at[1, k], (z, tm, to))

    def fold_3(k, source):
        to = lax.rem(hh + k, N)
        return remote(
            wth.at[hh], wth.at[source], wc_s.at[2, k], wc_r.at[2, k], (z, tm, to)
        )

    def fold_4(k, source):
        to = lax.rem(tm + k, N)
        return remote(
            wf.at[tm], wf.at[source], wc_s.at[3, k], wc_r.at[3, k], (z, to, hh)
        )

    go_each(lambda k: fold_1(k))

    def to_core(slot, part):
        return remote(
            part_of(xe.at[slot], part),
            part_of(xe.at[slot], part + 1),
            cc_s.at[slot, part // 2],
            cc_r.at[slot, part // 2],
            other_core,
        )

    def ring_part(step, part):
        def pass_on():
            z_right(step, part).wait_recv()
            if step < 4:
                z_right(step + 1, part).start()
                z_left(step, part).wait_recv()
            if step < 3:
                z_left(step + 1, part).start()

        def passed():
            if step < 4:
                z_right(step + 1, part).wait_send()
            if step < 3:
                z_left(step + 1, part).wait_send()

        if part in (1, 3):
            pl.when(first_core)(pass_on)
            sent.append(lambda: pl.when(first_core)(passed))
            return
        pass_on()
        sent.append(passed)
        go_if(first_core, lambda: to_core(2 * step - 1, part))
        if step < 4:
            go_if(first_core, lambda: to_core(2 * step, part))

    def core_arrived(slot):
        @pl.when(last_core)
        def _():
            if slot:
                to_core(slot, 0).wait_recv()
            to_core(slot, 2).wait_recv()

    halo_wait(0)

    @pl.when(jnp.logical_not(has_last))
    def _():
        first = xe[0, 2:3, 0:2]
        xe[0, 0:1, 0:2] = first
        xe[0, 1:2, 0:2] = first

    z_first(1)
    ring_part(1, 0)
    ring_part(1, 1)
    halo_wait(1)
    halo_wait(2)

    @pl.when(jnp.logical_not(has_down))
    def _():
        xe[0, 2:4, 2:3] = xe[0, 2:4, 0:1]

    @pl.when(jnp.logical_not(has_up))
    def _():
        xe[0, 2:4, 3:4] = xe[0, 2:4, 1:2]

    z_first(2)
    go_if(first_core, lambda: to_core(0, 2))
    halo_wait(3)
    halo_wait(4)

    @pl.when(jnp.logical_not(has_last))
    def _():
        first = xe[0, 2:3, 2:4]
        xe[0, 0:1, 2:4] = first
        xe[0, 1:2, 2:4] = first

    @pl.when(first_core & has_last & jnp.logical_not(has_down))
    def _():
        xe[0, 0:2, 2:3] = xe[0, 0:2, 0:1]

    @pl.when(first_core & has_last & jnp.logical_not(has_up))
    def _():
        xe[0, 0:2, 3:4] = xe[0, 0:2, 1:2]

    z_first(3)

    ring_part(2, 0)
    for k in y_order:
        y_copy(k, lax.rem(y + N - k, N)).wait_recv()
        for i in (1, 3, 2):
            go(x_copy(k, i, x))

    ring_part(2, 1)
    for part in (2, 3):
        ring_part(1, part)
    ring_part(3, 0)
    ring_part(3, 1)
    for part in (2, 3):
        ring_part(2, part)

    staged[5].wait()
    for ij in range(9):
        w2[16 * ij : 16 * ij + 16] = jnp.concatenate(
            [wo[3 * ij + l].astype(F32) for l in range(3)], axis=1
        ).astype(BF16)

    lane = iota((128, 512), 1)
    row = iota((128, 512), 0)
    s_at = (lane >> 6) & 3
    q_at = (lane >> 4) & 3
    f_at = (row >> 5) & 1
    r_at = (row >> 4) & 1
    in_frame = (s_at == f_at + 2) | ((tm == 0) & (s_at < 2) & (f_at == 0))
    in_row = (
        (q_at == r_at + 1)
        | ((hh == 0) & (q_at == 0) & (r_at == 0))
        | ((hh == N - 1) & (q_at == 3) & (r_at == 1))
    )
    same = ((lane & 15) == (row & 15)) & ((lane >> 8) == (row >> 6))
    place[...] = jnp.where(in_frame & in_row & same, 1.0, 0.0).astype(BF16)

    for copy in staged[6:]:
        copy.wait()
    entry = iota((16, 128), 1) >> 1
    token = iota((16, 128), 0)
    is_frame = entry < 8
    is_row = entry < 36
    start = jnp.where(is_frame, 0, jnp.where(is_row, 8, 36))
    width = jnp.where(is_frame, float(time_dims), float(row_dims))
    power = 2.0 * (entry - start).astype(F32) / width
    freq = jnp.exp(power * (-math.log(rope_base)))
    frame_at = jnp.where(token < 8, fp_ref[0].astype(F32), fp_ref[1].astype(F32))
    spot = jnp.where(
        is_frame,
        frame_at,
        jnp.where(is_row, rp_ref[0].astype(F32), (token & 7).astype(F32)),
    )
    angle = spot * freq
    odd = (iota((16, 128), 1) & 1) == 1
    cosine = jnp.cos(angle)
    sine = jnp.sin(angle)
    sine = jnp.where(odd, sine, -sine)
    for i, gain_of in enumerate((qg, kg)):
        gain_row = jnp.broadcast_to(gain_of[...].astype(F32), (16, 128))
        swapped = jnp.where(odd, pltpu.roll(gain_row, 1, 1), pltpu.roll(gain_row, 127, 1))
        trig_ref[2 * i] = cosine * gain_row
        trig_ref[2 * i + 1] = sine * swapped

    for k in (0,) + y_order:
        for i in range(1, 4):
            x_copy(k, i, lax.rem(x + 4 - i, 4)).wait_recv()
        go(core_copy(k, core))

    for part in (2, 3):
        ring_part(3, part)

    each(lambda k: fold_1(k).wait_recv())
    total = wp[pl.ds(8 * tm, 8)]
    for k in range(1, N):
        total = total + wr[k]
    wsum[...] = total
    go_each(lambda k: fold_2(k))

    for k in range(N):
        core_copy(k, 1 - core).wait_recv()

    def shard_of(index):
        t, h = index // N, index % N
        return wg[(h % 2) * 4 + t // 2, t % 2, h // 2]

    for tile in range(4 * TAPS):
        source, first = (128 * tile) // 216, (128 * tile) % 216
        count = min(128, 216 - first)
        value = shard_of(source)[:, first : first + count]
        if count < 128:
            value = jnp.concatenate([value, shard_of(source + 1)[:, : 128 - count]], axis=1)
        tap = tile // 4
        ij, l = tap // 3, tap % 3
        at = 128 * (tile % 4)
        bt[ij, 64 * l : 64 * l + 64, at : at + 128] = value

    col = iota((64, 128), 1) & 15

    def conv_pair(pair):
        total = jnp.zeros((192, 128), F32)
        for ij in range(9):
            i, j = ij // 3, ij % 3
            rows = [xe[2 * pair : 2 * pair + 2, i : i + 2, ROW[j + r]] for r in range(2)]
            block = jnp.stack(rows, axis=2).reshape(128, 512)
            total = total + lax.dot_general(bt[ij], block, NT, preferred_element_type=F32)
        left, mid, right = total[:64], total[64:128], total[128:]
        left = jnp.where(col == 0, left, pltpu.roll(left, 1, 1))
        right = jnp.where(col == 15, right, pltpu.roll(right, 127, 1))
        ht[pair] = left + mid + right

    for pair in range(3):
        core_arrived(2 * pair)
        core_arrived(2 * pair + 1)
        conv_pair(pair)
    for part in range(4):
        ring_part(4, part)
    core_arrived(6)
    core_arrived(7)
    conv_pair(3)

    stat_lane = iota((8, 128), 1)
    compact = jnp.zeros((8, 128), F32)
    for pair in range(4):
        value = ht[pair]
        sums = jnp.sum(value.reshape(4, 16, 128), axis=1)
        squares = jnp.sum((value * value).reshape(4, 16, 128), axis=1)
        both = jnp.concatenate([sums, squares], axis=0)
        low = jnp.sum(jnp.where(stat_lane < 64, both, 0.0), axis=1, keepdims=True)
        high = jnp.sum(jnp.where(stat_lane >= 64, both, 0.0), axis=1, keepdims=True)
        compact = jnp.where(stat_lane == pair, low, compact)
        compact = jnp.where(stat_lane == 64 + pair, high, compact)
    st[0, 0:1] = jnp.sum(pltpu.roll(compact, 0, 1, stride=4, stride_axis=0), axis=0, keepdims=True)

    def stat_copy(k):
        return remote(
            st.at[0, pl.ds(0, 1)], st.at[k, pl.ds(0, 1)], ss_s.at[k], ss_r.at[k], in_plane(k)
        )

    go_each(stat_copy, N * N)

    each(lambda k: fold_2(k).wait_recv())
    tile_sum = wsum[hh]
    for k in range(1, N):
        tile_sum = tile_sum + wrh[k]
    wth[hh] = tile_sum
    go_each(lambda k: fold_3(k, hh))

    diag = iota((64, 64), 0) == iota((64, 64), 1)
    gain = jnp.sum(jnp.where(diag, gg[...].astype(F32), 0.0), axis=1, keepdims=True)
    bias = jnp.sum(jnp.where(diag, gb[...].astype(F32), 0.0), axis=1, keepdims=True)
    diag = iota((16, 16), 0) == iota((16, 16), 1)
    out_bias = jnp.sum(jnp.where(diag, ob[...], 0.0), axis=1, keepdims=True)

    each(lambda k: stat_copy(k).wait_recv(), N * N)
    total = jnp.zeros((1, 128), F32)
    for k in range(N * N):
        total = total + st[k, 0:1]
    total = jnp.broadcast_to(total, (8, 128))
    compact = pltpu.roll(total, 100, 1, stride=4, stride_axis=0)
    count = float(16 * 16 * 16 * 16)
    average = compact / count
    mean = average
    var = pltpu.roll(average, 4, 0) - mean * mean
    inv = lax.rsqrt(var + norm_eps)

    wide = iota((16, 512), 1)
    t_at = (wide >> 6) & 3
    u_at = (wide >> 4) & 3
    lane_128 = iota((8, 128), 1)

    def spread(value, pair):
        lanes = jnp.where(
            lane_128 < 64,
            jnp.broadcast_to(value[:, pair : pair + 1], (8, 128)),
            jnp.broadcast_to(value[:, 64 + pair : 65 + pair], (8, 128)),
        )
        return jnp.concatenate(
            [jnp.broadcast_to(lanes[7 - g : 8 - g], (16, 128)) for g in range(4)], axis=0
        )

    def rz_copy(slot):
        to = lax.rem(z + N + SLOT_STEP[slot], N)
        return remote(outs.at[slot], rz.at[slot], rz_s.at[slot], rz_r.at[slot], (to, tm, hh))

    for pair in (3, 2, 1, 0):
        scale = spread(inv, pair) * gain
        offset = bias - spread(mean, pair) * scale
        value = ht[pair] * scale + offset
        value = value / (1.0 + jnp.exp(-value))
        left = jnp.where(col == 0, value, pltpu.roll(value, 1, 1))
        right = jnp.where(col == 15, value, pltpu.roll(value, 127, 1))
        stacked = jnp.concatenate([left, value, right], axis=0).astype(BF16)
        spots = jnp.dot(stacked, place[...], preferred_element_type=F32).astype(BF16)
        taps = jnp.dot(w2[...], spots, preferred_element_type=F32)
        total = jnp.zeros((16, 512), F32)
        for ij in range(9):
            i, j = ij // 3, ij % 3
            move = (16 * (1 - j) - 64 * i) % 512
            moved = taps[16 * ij : 16 * ij + 16]
            if move:
                moved = pltpu.roll(moved, move, 1)
            valid = t_at <= 3 - i
            if j == 0:
                valid = valid & (u_at >= 1)
            if j == 2:
                valid = valid & (u_at <= 2)
            total = total + jnp.where(valid, moved, 0.0)
        outs[2 * pair] = total[:, :256]
        outs[2 * pair + 1] = total[:, 256:]
        for slot in (2 * pair + 1, 2 * pair):
            if slot:
                go(rz_copy(slot))

    goes = (
        has_next,
        has_down,
        has_up,
        has_next & has_down,
        has_next & has_up,
    )
    comes = (
        has_last,
        has_up,
        has_down,
        has_last & has_up,
        has_last & has_down,
    )
    for i in range(5):

        @pl.when(jnp.logical_not(comes[i]))
        def _(i=i):
            rh[i] = jnp.zeros((16, 128), F32)

    each(lambda k: fold_3(k, lax.rem(hh + N - k, N)).wait_recv())
    wf[tm] = wth[...]
    go_each(lambda k: fold_4(k, tm))

    total = outs[0]
    for slot in range(1, N):
        rz_copy(slot).wait_recv()
        total = total + rz[slot]
    ext[0] = total[:, :128]
    ext[1] = total[:, 128:]

    def rh_copy(i):
        return remote(
            ext.at[1 if i in (0, 3, 4) else 0],
            rh.at[i],
            rh_s.at[i],
            rh_r.at[i],
            halos[i][2],
        )

    for i in range(5):
        go_if(goes[i], lambda i=i: rh_copy(i))
    for i in range(5):
        pl.when(comes[i])(lambda i=i: rh_copy(i).wait_recv())

    narrow = iota((16, 128), 1)
    u_at = (narrow >> 4) & 3
    inside = (u_at == 1) | (u_at == 2)
    latent = jnp.where(inside, total[:, :128] + rh[0], 0.0)
    latent = latent + jnp.where(u_at == 2, pltpu.roll(rh[1] + rh[3], 32, 1), 0.0)
    latent = latent + jnp.where(u_at == 1, pltpu.roll(rh[2] + rh[4], 96, 1), 0.0)
    latent = (latent + out_bias) * latent_scale

    lane = iota((128, 128), 1)
    group = (iota((128, 128), 0) >> 4) & 3
    keep = (((lane >> 4) & 3) == (group >> 1) + 1) & ((lane & 1) == (group & 1))
    rounded = latent.astype(BF16).astype(F32)
    many = jnp.where(keep, jnp.concatenate([rounded] * 8, axis=0), 0.0).astype(BF16)
    lane = iota((16, 128), 1)
    row = iota((16, 128), 0)
    pick = ((lane >> 6) == (row >> 3)) & (((lane & 15) >> 1) == (row & 7))
    pick = jnp.where(pick, 1.0, 0.0).astype(BF16)
    pb[z] = lax.dot_general(pick, many, NT, preferred_element_type=F32).astype(BF16)

    def pb_copy(k, source):
        return remote(
            pb.at[z],
            pb.at[source],
            pb_s.at[k],
            pb_r.at[k],
            (lax.rem(z + k, N), tm, hh),
        )

    go_each(lambda k: pb_copy(k, z))

    each(lambda k: fold_4(k, lax.rem(tm + N - k, N)).wait_recv())
    for lane_tile in range(6):
        for pair in range(4):
            tiles = [12 * pair + lane_tile, 12 * pair + 6 + lane_tile]
            value = jnp.concatenate([wf[t // 8, t % 8] for t in tiles], axis=0)
            high = value.astype(BF16)
            low = (value - high.astype(F32)).astype(BF16)
            at = slice(128 * lane_tile, 128 * lane_tile + 128)
            wcc_ref[16 * pair : 16 * pair + 16, at] = high
            wcc_ref[64 + 16 * pair : 64 + 16 * pair + 16, at] = low
    proj_bias = qb[...].astype(F32)
    bias_ref[...] = jnp.concatenate(
        [
            wf[6 + lane_tile // 8, lane_tile % 8][0:1] + proj_bias[lane_tile : lane_tile + 1]
            for lane_tile in range(6)
        ],
        axis=1,
    )

    lane = iota((256, 128), 1)
    row = iota((256, 128), 0)
    many = jnp.where((lane & 15) == (row >> 4), jnp.concatenate([latent] * 16, axis=0), 0.0)
    lane = iota((8, 128), 1)
    row = iota((8, 128), 0)
    pick = ((lane >> 6) == (row >> 1)) & (((lane >> 4) & 3) == (row & 1) + 1)
    pick = jnp.where(pick, 1.0, 0.0)
    lines = lax.dot_general(
        pick, many, NT, preferred_element_type=F32, precision=lax.Precision.HIGHEST
    )
    lat_ref[...] = lines[:4]

    each(lambda k: pb_copy(k, lax.rem(z + N - k, N)).wait_recv())
    pat_ref[...] = pb[...].reshape(128, 128)

    finish()


def project(lat_in, pat_ref, wcc_ref, bias_ref, trig_ref, lat_ref, q_ref, k_ref, v_ref):
    for row in range(4):
        lat_ref[0, row // 2, row % 2 : row % 2 + 1] = lat_in[row : row + 1]
    odd = (iota((128, 128), 1) & 1) == 1
    projected = jnp.dot(pat_ref[...], wcc_ref[...], preferred_element_type=F32)
    projected = projected + bias_ref[...]

    def turned(value, which):
        cosine = jnp.concatenate([trig_ref[2 * which]] * 8, axis=0)
        sine = jnp.concatenate([trig_ref[2 * which + 1]] * 8, axis=0)
        mean_square = jnp.mean(value * value, axis=1, keepdims=True)
        value = value * lax.rsqrt(mean_square + norm_eps)
        swapped = jnp.where(odd, pltpu.roll(value, 1, 1), pltpu.roll(value, 127, 1))
        return (value * cosine + swapped * sine).astype(BF16)

    for head in range(2):
        at = slice(HD * head, HD * head + HD)
        base = 3 * HD * head
        q_ref[:, at] = turned(projected[:, base : base + HD], 0)
        k_ref[:, at] = turned(projected[:, base + HD : base + 2 * HD], 1)
        v_ref[:, at] = projected[:, base + 2 * HD : base + 3 * HD].astype(BF16)


def shards(
    clip_inputs,
    conv_in_weight,
    group_gain,
    group_bias,
    conv_out_weight,
    out_bias,
    patch_weight,
    patch_bias,
    qkv_weight,
    qkv_bias,
    q_gain,
    k_gain,
    frame_pos,
    row_pos,
):
    vmem = pl.BlockSpec(memory_space=pltpu.VMEM)
    smem = pl.BlockSpec(memory_space=pltpu.SMEM)
    hbm = pl.BlockSpec(memory_space=pltpu.HBM)
    dma = pltpu.SemaphoreType.DMA
    travelled = pl.pallas_call(
        kernel,
        out_shape=(
            jax.ShapeDtypeStruct((4, 256), F32),
            jax.ShapeDtypeStruct((128, 128), BF16),
            jax.ShapeDtypeStruct((128, 768), BF16),
            jax.ShapeDtypeStruct((1, 768), F32),
            jax.ShapeDtypeStruct((4, 16, 128), F32),
        ),
        in_specs=[hbm] * 12 + [smem] * 2,
        out_specs=(vmem,) * 5,
        scratch_shapes=[
            pltpu.VMEM((N, 4, 4, 16, 512), BF16),
            pltpu.VMEM((64, 216), BF16),
            pltpu.VMEM((1, 64), BF16),
            pltpu.VMEM((1, 64), BF16),
            pltpu.VMEM((TAPS, 16, 64), BF16),
            pltpu.VMEM((1, 16), F32),
            pltpu.VMEM((64, 256), BF16),
            pltpu.VMEM((24, 128), BF16),
            pltpu.VMEM((48, 768), BF16),
            pltpu.VMEM((6, 128), BF16),
            pltpu.VMEM((1, 128), BF16),
            pltpu.VMEM((1, 128), BF16),
            pltpu.VMEM((N, 2, 4, 64, 256), BF16),
            pltpu.VMEM((9, 192, 512), BF16),
            pltpu.VMEM((4, 64, 128), F32),
            pltpu.VMEM((144, 192), BF16),
            pltpu.VMEM((128, 512), BF16),
            pltpu.VMEM((64, 8, 128), F32),
            pltpu.VMEM((N, 8, 8, 128), F32),
            pltpu.VMEM((8, 8, 128), F32),
            pltpu.VMEM((N, 8, 128), F32),
            pltpu.VMEM((N, 8, 128), F32),
            pltpu.VMEM((N, 8, 8, 128), F32),
            pltpu.VMEM((N * N, 8, 128), F32),
            pltpu.VMEM((N, 16, 256), F32),
            pltpu.VMEM((N, 16, 256), F32),
            pltpu.VMEM((2, 16, 128), F32),
            pltpu.VMEM((5, 16, 128), F32),
            pltpu.VMEM((N, 16, 128), BF16),
            dma((12,)),
            dma((4, 4)),
            dma((4, 4)),
            dma((3, 4)),
            dma((3, 4)),
            dma((5,)),
            dma((5,)),
            dma((N, 2)),
            dma((N, 2)),
            dma((N,)),
            dma((N,)),
            dma((N, 4)),
            dma((N, 4)),
            dma((N,)),
            dma((N,)),
            dma((4, N)),
            dma((4, N)),
            dma((N * N,)),
            dma((N * N,)),
            dma((N,)),
            dma((N,)),
            dma((5,)),
            dma((5,)),
            dma((N,)),
            dma((N,)),
        ],
        compiler_params=pltpu.CompilerParams(
            collective_id=0, has_side_effects=True, vmem_limit_bytes=63 * 2**20
        ),
    )(
        clip_inputs[0],
        conv_in_weight.T,
        group_gain[None],
        group_bias[None],
        conv_out_weight.transpose(0, 2, 1),
        out_bias[None],
        patch_weight,
        patch_bias.reshape(24, 128),
        qkv_weight,
        qkv_bias.reshape(6, 128),
        q_gain[None],
        k_gain[None],
        frame_pos,
        row_pos,
    )
    latents, queries, keys, values = pl.pallas_call(
        project,
        out_shape=(
            jax.ShapeDtypeStruct((1, 2, 2, 256), F32),
            jax.ShapeDtypeStruct((128, 256), BF16),
            jax.ShapeDtypeStruct((128, 256), BF16),
            jax.ShapeDtypeStruct((128, 256), BF16),
        ),
        in_specs=[vmem] * 5,
        out_specs=(vmem,) * 4,
    )(*travelled)
    merged = (N, 2, 1, 8, 2 * HD)
    return (
        latents,
        queries.reshape(merged),
        keys.reshape(merged),
        values.reshape(merged),
    )


def solution(mesh):
    placed = (
        P("dp", "tm", "height", None, None),
        P(("tm", "height"), "dp"),
        P("dp"),
        P("dp"),
        P(None, "dp", None),
        P(),
        P(),
        P(),
        P(("tm", "height"), "dp"),
        P("dp"),
        P(),
        P(),
        P("tm"),
        P("height"),
    )
    return jax.shard_map(
        shards,
        mesh=mesh,
        in_specs=placed,
        out_specs=(
            P("dp", "tm", "height", None),
            P(None, "tm", "height", None, "dp"),
            P(None, "tm", "height", None, "dp"),
            P(None, "tm", "height", None, "dp"),
        ),
        check_vma=False,
    )
```

```python
import math

import jax
import jax.numpy as jnp
from jax import lax
from jax.experimental import pallas as pl
from jax.experimental.pallas import tpu as pltpu
from jax.sharding import PartitionSpec as P

HD = 128
GROUPS = 32
TAPS = 27
N = 8

norm_eps = 1e-06
latent_scale = 0.476986
rope_base = 256.0
time_dims = 16
row_dims = 56

F32 = jnp.float32
BF16 = jnp.bfloat16
MESH = pl.DeviceIdType.MESH

SLOT_STEP = (0, -1, 1, -2, 2, -3, 3, -4)

ROW = (2, 0, 1, 3)

NT = (((1,), (1,)), ((), ()))


def iota(shape, dim):
    return lax.broadcasted_iota(jnp.int32, shape, dim)


def part_of(ref, which):
    frames, rows = ((2, 0), (0, 0), (2, 2), (0, 2))[which]
    return ref.at[pl.ds(frames, 2), pl.ds(rows, 2)]


def kernel(
    x_ref,
    wi_ref,
    gg_ref,
    gb_ref,
    wo_ref,
    ob_ref,
    pw_ref,
    pb_ref,
    qw_ref,
    qb_ref,
    qg_ref,
    kg_ref,
    fp_ref,
    rp_ref,
    lat_ref,
    pat_ref,
    wcc_ref,
    bias_ref,
    trig_ref,
    xe,
    wi,
    gg,
    gb,
    wo,
    ob,
    pw,
    pbias,
    qw,
    qb,
    qg,
    kg,
    wg,
    bt,
    ht,
    w2,
    place,
    wp,
    wr,
    wsum,
    wrh,
    wth,
    wf,
    st,
    outs,
    rz,
    ext,
    rh,
    pb,
    in_sem,
    zr_s,
    zr_r,
    zl_s,
    zl_r,
    ha_s,
    ha_r,
    cc_s,
    cc_r,
    wy_s,
    wy_r,
    wx_s,
    wx_r,
    co_s,
    co_r,
    wc_s,
    wc_r,
    ss_s,
    ss_r,
    rz_s,
    rz_r,
    rh_s,
    rh_r,
    pb_s,
    pb_r,
):
    z = lax.axis_index("dp")
    tm = lax.axis_index("tm")
    hh = lax.axis_index("height")
    core = lax.rem(tm, 2)
    y_lo = tm // 2
    x = hh // 2
    y_hi = lax.rem(hh, 2)
    y = y_hi * 4 + y_lo

    def at_y(where):
        return (z, lax.rem(where, 4) * 2 + core, x * 2 + where // 4)

    def remote(src, dst, send, recv, device):
        return pltpu.make_async_remote_copy(
            src_ref=src,
            dst_ref=dst,
            send_sem=send,
            recv_sem=recv,
            device_id=device,
            device_id_type=MESH,
        )

    sent = []

    def go(copy):
        copy.start()
        sent.append(copy.wait_send)

    def go_if(condition, make):
        pl.when(condition)(lambda: make().start())
        sent.append(lambda: pl.when(condition)(lambda: make().wait_send()))

    def each(fn, end=N):
        def body(k, _):
            fn(k)
            return 0

        lax.fori_loop(1, end, body, 0)

    def go_each(make, end=N):
        each(lambda k: make(k).start(), end)
        sent.append(lambda: each(lambda k: make(k).wait_send(), end))

    def finish(keep=0):
        while len(sent) > keep:
            sent.pop(0)()

    z_up = (lax.rem(z + 1, N), tm, hh)
    z_down = (lax.rem(z + N - 1, N), tm, hh)
    other_core = (z, tm + 1 - 2 * core, hh)
    first_core = core == 0
    last_core = core == 1

    barrier = pltpu.get_barrier_semaphore()

    def greet(device):
        pl.semaphore_signal(barrier, inc=1, device_id=device, device_id_type=MESH)

    def in_plane(k):
        return (z, lax.rem(tm + k // N, N), lax.rem(hh + lax.rem(k, N), N))

    each(lambda k: greet((lax.rem(z + k, N), tm, hh)))
    each(lambda k: greet(in_plane(k)), N * N)

    d = tm * N + hh
    tile = jnp.minimum(48 * d // 128, 22)
    shift = 48 * d - 128 * tile
    window = pl.ds(pl.multiple_of(tile * 128, 128), 256)
    own = xe.at[0]
    staged = [
        (wi_ref, wi),
        (x_ref, part_of(own, 0)),
        (pw_ref.at[:, window], pw),
        (pb_ref, pbias),
        (qw_ref, qw),
        (wo_ref, wo),
        (gg_ref, gg),
        (gb_ref, gb),
        (ob_ref, ob),
        (qb_ref, qb),
        (qg_ref, qg),
        (kg_ref, kg),
    ]
    staged = [
        pltpu.make_async_copy(src, dst, in_sem.at[i]) for i, (src, dst) in enumerate(staged)
    ]
    for copy in staged:
        copy.start()

    wg[y, core, x] = jnp.zeros((64, 256), BF16)
    staged[0].wait()
    wg[y, core, x, :, pl.ds(0, 216)] = wi[...]
    staged[1].wait()

    pl.semaphore_wait(barrier, N - 1 + N * N - 1)

    def z_right(step, part):
        return remote(
            part_of(xe.at[SLOT_STEP.index(1 - step)], part),
            part_of(xe.at[SLOT_STEP.index(-step)], part),
            zr_s.at[step - 1, part],
            zr_r.at[step - 1, part],
            z_up,
        )

    def z_left(step, part):
        return remote(
            part_of(xe.at[SLOT_STEP.index(step - 1)], part),
            part_of(xe.at[SLOT_STEP.index(step)], part),
            zl_s.at[step - 1, part],
            zl_r.at[step - 1, part],
            z_down,
        )

    def z_first(part):
        if part in (0, 2):
            go(z_right(1, part))
            go(z_left(1, part))
        else:
            go_if(first_core, lambda: z_right(1, part))
            go_if(first_core, lambda: z_left(1, part))

    has_next = tm < N - 1
    has_last = tm > 0
    has_up = hh < N - 1
    has_down = hh > 0
    next_tm = lax.rem(tm + 1, N)
    up_h = lax.rem(hh + 1, N)
    down_h = lax.rem(hh + N - 1, N)
    row_0 = own.at[pl.ds(2, 2), pl.ds(0, 1)]
    row_1 = own.at[pl.ds(2, 2), pl.ds(1, 1)]
    halos = (
        (part_of(own, 0), part_of(own, 1), (z, next_tm, hh), has_next, has_last),
        (row_0, own.at[pl.ds(2, 2), pl.ds(3, 1)], (z, tm, down_h), has_down, has_up),
        (row_1, own.at[pl.ds(2, 2), pl.ds(2, 1)], (z, tm, up_h), has_up, has_down),
        (
            row_0,
            own.at[pl.ds(0, 2), pl.ds(3, 1)],
            (z, next_tm, down_h),
            last_core & has_next & has_down,
            first_core & has_last & has_up,
        ),
        (
            row_1,
            own.at[pl.ds(0, 2), pl.ds(2, 1)],
            (z, next_tm, up_h),
            last_core & has_next & has_up,
            first_core & has_last & has_down,
        ),
    )

    def halo_copy(i):
        src, dst, device, _, _ = halos[i]
        return remote(src, dst, ha_s.at[i], ha_r.at[i], device)

    def halo_wait(i):
        pl.when(halos[i][4])(lambda: halo_copy(i).wait_recv())

    for i in (3, 4, 1, 2, 0):
        go_if(halos[i][3], lambda i=i: halo_copy(i))
    z_first(0)

    def y_copy(k, source):
        return remote(
            wg.at[y, core, x],
            wg.at[source, core, x],
            wy_s.at[k],
            wy_r.at[k],
            at_y(lax.rem(y + k, N)),
        )

    def x_copy(k, i, source):
        line = lax.rem(y + N - k, N)
        return remote(
            wg.at[line, core, x],
            wg.at[line, core, source],
            wx_s.at[k, i],
            wx_r.at[k, i],
            (z, tm, lax.rem(hh + 2 * i, N)),
        )

    def core_copy(k, source):
        line = lax.rem(y + N - k, N)
        return remote(
            wg.at[line, core], wg.at[line, source], co_s.at[k], co_r.at[k], other_core
        )

    y_order = (1, 7, 2, 6, 3, 5, 4)
    for k in y_order:
        go(y_copy(k, y))
    for i in (1, 3, 2):
        go(x_copy(0, i, x))

    for copy in staged[2:5]:
        copy.wait()
    bias_rows = pbias[...].astype(F32)
    bias_tile = iota((24, 128), 0)
    bias_row = jnp.concatenate(
        [
            jnp.sum(jnp.where(bias_tile == tile + i, bias_rows, 0.0), axis=0, keepdims=True)
            for i in range(2)
        ],
        axis=1,
    )
    embed = jnp.concatenate([pw[...].astype(F32), jnp.broadcast_to(bias_row, (8, 256))], axis=0)
    embed = pltpu.roll(embed, lax.rem(256 - shift, 256), 1)[:, :48].astype(BF16)
    part = jnp.dot(embed, qw[...], preferred_element_type=F32)
    for row in range(9):
        for lane in range(6):
            wp[row * 6 + lane] = part[8 * row : 8 * row + 8, 128 * lane : 128 * lane + 128]
    wp[pl.ds(54, 10)] = jnp.zeros((10, 8, 128), F32)

    def fold_1(k):
        to = lax.rem(tm + k, N)
        return remote(
            wp.at[pl.ds(8 * to, 8)], wr.at[k], wc_s.at[0, k], wc_r.at[0, k], (z, to, hh)
        )

    def fold_2(k):
        to = lax.rem(hh + k, N)
        return remote(wsum.at[to], wrh.at[k], wc_s.at[1, k], wc_r.at[1, k], (z, tm, to))

    def fold_3(k, source):
        to = lax.rem(hh + k, N)
        return remote(
            wth.at[hh], wth.at[source], wc_s.at[2, k], wc_r.at[2, k], (z, tm, to)
        )

    def fold_4(k, source):
        to = lax.rem(tm + k, N)
        return remote(
            wf.at[tm], wf.at[source], wc_s.at[3, k], wc_r.at[3, k], (z, to, hh)
        )

    def to_core(slot, part):
        return remote(
            part_of(xe.at[slot], part),
            part_of(xe.at[slot], part + 1),
            cc_s.at[slot, part // 2],
            cc_r.at[slot, part // 2],
            other_core,
        )

    def ring_part(step, part):
        def pass_on():
            z_right(step, part).wait_recv()
            if step < 4:
                z_right(step + 1, part).start()
                z_left(step, part).wait_recv()
            if step < 3:
                z_left(step + 1, part).start()

        def passed():
            if step < 4:
                z_right(step + 1, part).wait_send()
            if step < 3:
                z_left(step + 1, part).wait_send()

        if part in (1, 3):
            pl.when(first_core)(pass_on)
            sent.append(lambda: pl.when(first_core)(passed))
            return
        pass_on()
        sent.append(passed)
        go_if(first_core, lambda: to_core(2 * step - 1, part))
        if step < 4:
            go_if(first_core, lambda: to_core(2 * step, part))

    def core_arrived(slot):
        @pl.when(last_core)
        def _():
            if slot:
                to_core(slot, 0).wait_recv()
            to_core(slot, 2).wait_recv()

    halo_wait(0)

    @pl.when(jnp.logical_not(has_last))
    def _():
        first = xe[0, 2:3, 0:2]
        xe[0, 0:1, 0:2] = first
        xe[0, 1:2, 0:2] = first

    z_first(1)
    ring_part(1, 0)
    ring_part(1, 1)
    halo_wait(1)
    halo_wait(2)

    @pl.when(jnp.logical_not(has_down))
    def _():
        xe[0, 2:4, 2:3] = xe[0, 2:4, 0:1]

    @pl.when(jnp.logical_not(has_up))
    def _():
        xe[0, 2:4, 3:4] = xe[0, 2:4, 1:2]

    z_first(2)
    go_if(first_core, lambda: to_core(0, 2))
    halo_wait(3)
    halo_wait(4)

    @pl.when(jnp.logical_not(has_last))
    def _():
        first = xe[0, 2:3, 2:4]
        xe[0, 0:1, 2:4] = first
        xe[0, 1:2, 2:4] = first

    @pl.when(first_core & has_last & jnp.logical_not(has_down))
    def _():
        xe[0, 0:2, 2:3] = xe[0, 0:2, 0:1]

    @pl.when(first_core & has_last & jnp.logical_not(has_up))
    def _():
        xe[0, 0:2, 3:4] = xe[0, 0:2, 1:2]

    z_first(3)

    ring_part(2, 0)
    for k in y_order:
        y_copy(k, lax.rem(y + N - k, N)).wait_recv()
        for i in (1, 3, 2):
            go(x_copy(k, i, x))

    ring_part(2, 1)
    for part in (2, 3):
        ring_part(1, part)
    go_each(lambda k: fold_1(k))
    ring_part(3, 0)
    ring_part(3, 1)
    for part in (2, 3):
        ring_part(2, part)

    for k in (0,) + y_order:
        for i in range(1, 4):
            x_copy(k, i, lax.rem(x + 4 - i, 4)).wait_recv()
        go(core_copy(k, core))

    for part in (2, 3):
        ring_part(3, part)

    each(lambda k: fold_1(k).wait_recv())
    total = wp[pl.ds(8 * tm, 8)]
    for k in range(1, N):
        total = total + wr[k]
    wsum[...] = total
    go_each(lambda k: fold_2(k))

    for k in range(N):
        core_copy(k, 1 - core).wait_recv()

    def shard_of(index):
        t, h = index // N, index % N
        return wg[(h % 2) * 4 + t // 2, t % 2, h // 2]

    for tile in range(4 * TAPS):
        source, first = (128 * tile) // 216, (128 * tile) % 216
        count = min(128, 216 - first)
        value = shard_of(source)[:, first : first + count]
        if count < 128:
            value = jnp.concatenate([value, shard_of(source + 1)[:, : 128 - count]], axis=1)
        tap = tile // 4
        ij, l = tap // 3, tap % 3
        at = 128 * (tile % 4)
        bt[ij, 64 * l : 64 * l + 64, at : at + 128] = value

    col = iota((64, 128), 1) & 15

    def conv_pair(pair):
        total = jnp.zeros((192, 128), F32)
        for ij in range(9):
            i, j = ij // 3, ij % 3
            rows = [xe[2 * pair : 2 * pair + 2, i : i + 2, ROW[j + r]] for r in range(2)]
            block = jnp.stack(rows, axis=2).reshape(128, 512)
            total = total + lax.dot_general(bt[ij], block, NT, preferred_element_type=F32)
        left, mid, right = total[:64], total[64:128], total[128:]
        left = jnp.where(col == 0, left, pltpu.roll(left, 1, 1))
        right = jnp.where(col == 15, right, pltpu.roll(right, 127, 1))
        ht[pair] = left + mid + right

    for pair in range(3):
        core_arrived(2 * pair)
        core_arrived(2 * pair + 1)
        conv_pair(pair)
    for part in range(4):
        ring_part(4, part)
    core_arrived(6)
    core_arrived(7)
    conv_pair(3)

    stat_lane = iota((8, 128), 1)
    compact = jnp.zeros((8, 128), F32)
    for pair in range(4):
        value = ht[pair]
        sums = jnp.sum(value.reshape(4, 16, 128), axis=1)
        squares = jnp.sum((value * value).reshape(4, 16, 128), axis=1)
        both = jnp.concatenate([sums, squares], axis=0)
        low = jnp.sum(jnp.where(stat_lane < 64, both, 0.0), axis=1, keepdims=True)
        high = jnp.sum(jnp.where(stat_lane >= 64, both, 0.0), axis=1, keepdims=True)
        compact = jnp.where(stat_lane == pair, low, compact)
        compact = jnp.where(stat_lane == 64 + pair, high, compact)
    st[0:1] = jnp.sum(pltpu.roll(compact, 0, 1, stride=4, stride_axis=0), axis=0, keepdims=True)

    def stat_copy(k):
        return remote(st.at[pl.ds(0, 1)], st.at[pl.ds(k, 1)], ss_s, ss_r, in_plane(k))

    each(lambda k: stat_copy(k).start(), N * N)
    others = st.at[pl.ds(1, N * N - 1)]
    finish()

    for copy in staged[5:]:
        copy.wait()
    for ij in range(9):
        w2[16 * ij : 16 * ij + 16] = jnp.concatenate(
            [wo[3 * ij + l].astype(F32) for l in range(3)], axis=1
        ).astype(BF16)

    lane = iota((128, 512), 1)
    row = iota((128, 512), 0)
    s_at = (lane >> 6) & 3
    q_at = (lane >> 4) & 3
    f_at = (row >> 5) & 1
    r_at = (row >> 4) & 1
    in_frame = (s_at == f_at + 2) | ((tm == 0) & (s_at < 2) & (f_at == 0))
    in_row = (
        (q_at == r_at + 1)
        | ((hh == 0) & (q_at == 0) & (r_at == 0))
        | ((hh == N - 1) & (q_at == 3) & (r_at == 1))
    )
    same = ((lane & 15) == (row & 15)) & ((lane >> 8) == (row >> 6))
    place[...] = jnp.where(in_frame & in_row & same, 1.0, 0.0).astype(BF16)

    each(lambda k: fold_2(k).wait_recv())
    tile_sum = wsum[hh]
    for k in range(1, N):
        tile_sum = tile_sum + wrh[k]
    wth[hh] = tile_sum
    go_each(lambda k: fold_3(k, hh))

    diag = iota((64, 64), 0) == iota((64, 64), 1)
    gain = jnp.sum(jnp.where(diag, gg[...].astype(F32), 0.0), axis=1, keepdims=True)
    bias = jnp.sum(jnp.where(diag, gb[...].astype(F32), 0.0), axis=1, keepdims=True)
    diag = iota((16, 16), 0) == iota((16, 16), 1)
    out_bias = jnp.sum(jnp.where(diag, ob[...], 0.0), axis=1, keepdims=True)

    remote(others, others, ss_s, ss_r, in_plane(1)).wait()
    total = jnp.broadcast_to(jnp.sum(st[...], axis=0, keepdims=True), (8, 128))
    compact = pltpu.roll(total, 100, 1, stride=4, stride_axis=0)
    count = float(16 * 16 * 16 * 16)
    average = compact / count
    mean = average
    var = pltpu.roll(average, 4, 0) - mean * mean
    inv = lax.rsqrt(var + norm_eps)

    wide = iota((16, 512), 1)
    t_at = (wide >> 6) & 3
    u_at = (wide >> 4) & 3
    lane_128 = iota((8, 128), 1)

    def spread(value, pair):
        lanes = jnp.where(
            lane_128 < 64,
            jnp.broadcast_to(value[:, pair : pair + 1], (8, 128)),
            jnp.broadcast_to(value[:, 64 + pair : 65 + pair], (8, 128)),
        )
        return jnp.concatenate(
            [jnp.broadcast_to(lanes[7 - g : 8 - g], (16, 128)) for g in range(4)], axis=0
        )

    def rz_copy(slot):
        to = lax.rem(z + N + SLOT_STEP[slot], N)
        return remote(outs.at[slot], rz.at[slot], rz_s.at[slot], rz_r.at[slot], (to, tm, hh))

    for pair in (3, 2, 1, 0):
        scale = spread(inv, pair) * gain
        offset = bias - spread(mean, pair) * scale
        value = ht[pair] * scale + offset
        value = value / (1.0 + jnp.exp(-value))
        left = jnp.where(col == 0, value, pltpu.roll(value, 1, 1))
        right = jnp.where(col == 15, value, pltpu.roll(value, 127, 1))
        stacked = jnp.concatenate([left, value, right], axis=0).astype(BF16)
        spots = jnp.dot(stacked, place[...], preferred_element_type=F32).astype(BF16)
        taps = jnp.dot(w2[...], spots, preferred_element_type=F32)
        total = jnp.zeros((16, 512), F32)
        for ij in range(9):
            i, j = ij // 3, ij % 3
            move = (16 * (1 - j) - 64 * i) % 512
            moved = taps[16 * ij : 16 * ij + 16]
            if move:
                moved = pltpu.roll(moved, move, 1)
            valid = t_at <= 3 - i
            if j == 0:
                valid = valid & (u_at >= 1)
            if j == 2:
                valid = valid & (u_at <= 2)
            total = total + jnp.where(valid, moved, 0.0)
        outs[2 * pair] = total[:, :256]
        outs[2 * pair + 1] = total[:, 256:]
        for slot in (2 * pair + 1, 2 * pair):
            if slot:
                go(rz_copy(slot))

    goes = (
        has_next,
        has_down,
        has_up,
        has_next & has_down,
        has_next & has_up,
    )
    comes = (
        has_last,
        has_up,
        has_down,
        has_last & has_up,
        has_last & has_down,
    )
    for i in range(5):

        @pl.when(jnp.logical_not(comes[i]))
        def _(i=i):
            rh[i] = jnp.zeros((16, 128), F32)

    each(lambda k: fold_3(k, lax.rem(hh + N - k, N)).wait_recv())
    wf[tm] = wth[...]
    go_each(lambda k: fold_4(k, tm))

    finish(7)

    entry = iota((16, 128), 1) >> 1
    token = iota((16, 128), 0)
    is_frame = entry < 8
    is_row = entry < 36
    start = jnp.where(is_frame, 0, jnp.where(is_row, 8, 36))
    width = jnp.where(is_frame, float(time_dims), float(row_dims))
    power = 2.0 * (entry - start).astype(F32) / width
    freq = jnp.exp(power * (-math.log(rope_base)))
    frame_at = jnp.where(token < 8, fp_ref[0].astype(F32), fp_ref[1].astype(F32))
    spot = jnp.where(
        is_frame,
        frame_at,
        jnp.where(is_row, rp_ref[0].astype(F32), (token & 7).astype(F32)),
    )
    angle = spot * freq
    odd = (iota((16, 128), 1) & 1) == 1
    cosine = jnp.cos(angle)
    sine = jnp.sin(angle)
    sine = jnp.where(odd, sine, -sine)
    for i, gain_of in enumerate((qg, kg)):
        gain_row = jnp.broadcast_to(gain_of[...].astype(F32), (16, 128))
        swapped = jnp.where(odd, pltpu.roll(gain_row, 1, 1), pltpu.roll(gain_row, 127, 1))
        trig_ref[2 * i] = cosine * gain_row
        trig_ref[2 * i + 1] = sine * swapped

    total = outs[0]
    for slot in range(1, N):
        rz_copy(slot).wait_recv()
        total = total + rz[slot]
    ext[0] = total[:, :128]
    ext[1] = total[:, 128:]

    def rh_copy(i):
        return remote(
            ext.at[1 if i in (0, 3, 4) else 0],
            rh.at[i],
            rh_s.at[i],
            rh_r.at[i],
            halos[i][2],
        )

    for i in range(5):
        go_if(goes[i], lambda i=i: rh_copy(i))
    for i in range(5):
        pl.when(comes[i])(lambda i=i: rh_copy(i).wait_recv())

    narrow = iota((16, 128), 1)
    u_at = (narrow >> 4) & 3
    inside = (u_at == 1) | (u_at == 2)
    latent = jnp.where(inside, total[:, :128] + rh[0], 0.0)
    latent = latent + jnp.where(u_at == 2, pltpu.roll(rh[1] + rh[3], 32, 1), 0.0)
    latent = latent + jnp.where(u_at == 1, pltpu.roll(rh[2] + rh[4], 96, 1), 0.0)
    latent = (latent + out_bias) * latent_scale

    lane = iota((128, 128), 1)
    group = (iota((128, 128), 0) >> 4) & 3
    keep = (((lane >> 4) & 3) == (group >> 1) + 1) & ((lane & 1) == (group & 1))
    rounded = latent.astype(BF16).astype(F32)
    many = jnp.where(keep, jnp.concatenate([rounded] * 8, axis=0), 0.0).astype(BF16)
    lane = iota((16, 128), 1)
    row = iota((16, 128), 0)
    pick = ((lane >> 6) == (row >> 3)) & (((lane & 15) >> 1) == (row & 7))
    pick = jnp.where(pick, 1.0, 0.0).astype(BF16)
    pb[z] = lax.dot_general(pick, many, NT, preferred_element_type=F32).astype(BF16)

    def pb_copy(k, source):
        return remote(
            pb.at[z],
            pb.at[source],
            pb_s.at[k],
            pb_r.at[k],
            (lax.rem(z + k, N), tm, hh),
        )

    go_each(lambda k: pb_copy(k, z))
    finish(1)

    each(lambda k: fold_4(k, lax.rem(tm + N - k, N)).wait_recv())
    for lane_tile in range(6):
        for pair in range(4):
            tiles = [12 * pair + lane_tile, 12 * pair + 6 + lane_tile]
            value = jnp.concatenate([wf[t // 8, t % 8] for t in tiles], axis=0)
            high = value.astype(BF16)
            low = (value - high.astype(F32)).astype(BF16)
            at = slice(128 * lane_tile, 128 * lane_tile + 128)
            wcc_ref[16 * pair : 16 * pair + 16, at] = high
            wcc_ref[64 + 16 * pair : 64 + 16 * pair + 16, at] = low
    proj_bias = qb[...].astype(F32)
    bias_ref[...] = jnp.concatenate(
        [
            wf[6 + lane_tile // 8, lane_tile % 8][0:1] + proj_bias[lane_tile : lane_tile + 1]
            for lane_tile in range(6)
        ],
        axis=1,
    )

    lane = iota((256, 128), 1)
    row = iota((256, 128), 0)
    many = jnp.where((lane & 15) == (row >> 4), jnp.concatenate([latent] * 16, axis=0), 0.0)
    lane = iota((8, 128), 1)
    row = iota((8, 128), 0)
    pick = ((lane >> 6) == (row >> 1)) & (((lane >> 4) & 3) == (row & 1) + 1)
    pick = jnp.where(pick, 1.0, 0.0)
    lines = lax.dot_general(
        pick, many, NT, preferred_element_type=F32, precision=lax.Precision.HIGHEST
    )
    lat_ref[...] = lines[:4]

    each(lambda k: pb_copy(k, lax.rem(z + N - k, N)).wait_recv())
    pat_ref[...] = pb[...].reshape(128, 128)

    finish()


def project(lat_in, pat_ref, wcc_ref, bias_ref, trig_ref, lat_ref, q_ref, k_ref, v_ref):
    for row in range(4):
        lat_ref[0, row // 2, row % 2 : row % 2 + 1] = lat_in[row : row + 1]
    odd = (iota((128, 128), 1) & 1) == 1
    projected = jnp.dot(pat_ref[...], wcc_ref[...], preferred_element_type=F32)
    projected = projected + bias_ref[...]

    def turned(value, which):
        cosine = jnp.concatenate([trig_ref[2 * which]] * 8, axis=0)
        sine = jnp.concatenate([trig_ref[2 * which + 1]] * 8, axis=0)
        mean_square = jnp.mean(value * value, axis=1, keepdims=True)
        value = value * lax.rsqrt(mean_square + norm_eps)
        swapped = jnp.where(odd, pltpu.roll(value, 1, 1), pltpu.roll(value, 127, 1))
        return (value * cosine + swapped * sine).astype(BF16)

    for head in range(2):
        at = slice(HD * head, HD * head + HD)
        base = 3 * HD * head
        q_ref[:, at] = turned(projected[:, base : base + HD], 0)
        k_ref[:, at] = turned(projected[:, base + HD : base + 2 * HD], 1)
        v_ref[:, at] = projected[:, base + 2 * HD : base + 3 * HD].astype(BF16)


def shards(
    clip_inputs,
    conv_in_weight,
    group_gain,
    group_bias,
    conv_out_weight,
    out_bias,
    patch_weight,
    patch_bias,
    qkv_weight,
    qkv_bias,
    q_gain,
    k_gain,
    frame_pos,
    row_pos,
):
    vmem = pl.BlockSpec(memory_space=pltpu.VMEM)
    smem = pl.BlockSpec(memory_space=pltpu.SMEM)
    hbm = pl.BlockSpec(memory_space=pltpu.HBM)
    dma = pltpu.SemaphoreType.DMA
    travelled = pl.pallas_call(
        kernel,
        out_shape=(
            jax.ShapeDtypeStruct((4, 256), F32),
            jax.ShapeDtypeStruct((128, 128), BF16),
            jax.ShapeDtypeStruct((128, 768), BF16),
            jax.ShapeDtypeStruct((1, 768), F32),
            jax.ShapeDtypeStruct((4, 16, 128), F32),
        ),
        in_specs=[hbm] * 12 + [smem] * 2,
        out_specs=(vmem,) * 5,
        scratch_shapes=[
            pltpu.VMEM((N, 4, 4, 16, 512), BF16),
            pltpu.VMEM((64, 216), BF16),
            pltpu.VMEM((1, 64), BF16),
            pltpu.VMEM((1, 64), BF16),
            pltpu.VMEM((TAPS, 16, 64), BF16),
            pltpu.VMEM((1, 16), F32),
            pltpu.VMEM((64, 256), BF16),
            pltpu.VMEM((24, 128), BF16),
            pltpu.VMEM((48, 768), BF16),
            pltpu.VMEM((6, 128), BF16),
            pltpu.VMEM((1, 128), BF16),
            pltpu.VMEM((1, 128), BF16),
            pltpu.VMEM((N, 2, 4, 64, 256), BF16),
            pltpu.VMEM((9, 192, 512), BF16),
            pltpu.VMEM((4, 64, 128), F32),
            pltpu.VMEM((144, 192), BF16),
            pltpu.VMEM((128, 512), BF16),
            pltpu.VMEM((64, 8, 128), F32),
            pltpu.VMEM((N, 8, 8, 128), F32),
            pltpu.VMEM((8, 8, 128), F32),
            pltpu.VMEM((N, 8, 128), F32),
            pltpu.VMEM((N, 8, 128), F32),
            pltpu.VMEM((N, 8, 8, 128), F32),
            pltpu.VMEM((N * N, 128), F32),
            pltpu.VMEM((N, 16, 256), F32),
            pltpu.VMEM((N, 16, 256), F32),
            pltpu.VMEM((2, 16, 128), F32),
            pltpu.VMEM((5, 16, 128), F32),
            pltpu.VMEM((N, 16, 128), BF16),
            dma((12,)),
            dma((4, 4)),
            dma((4, 4)),
            dma((3, 4)),
            dma((3, 4)),
            dma((5,)),
            dma((5,)),
            dma((N, 2)),
            dma((N, 2)),
            dma((N,)),
            dma((N,)),
            dma((N, 4)),
            dma((N, 4)),
            dma((N,)),
            dma((N,)),
            dma((4, N)),
            dma((4, N)),
            dma,
            dma,
            dma((N,)),
            dma((N,)),
            dma((5,)),
            dma((5,)),
            dma((N,)),
            dma((N,)),
        ],
        compiler_params=pltpu.CompilerParams(
            collective_id=0, has_side_effects=True, vmem_limit_bytes=63 * 2**20
        ),
    )(
        clip_inputs[0],
        conv_in_weight.T,
        group_gain[None],
        group_bias[None],
        conv_out_weight.transpose(0, 2, 1),
        out_bias[None],
        patch_weight,
        patch_bias.reshape(24, 128),
        qkv_weight,
        qkv_bias.reshape(6, 128),
        q_gain[None],
        k_gain[None],
        frame_pos,
        row_pos,
    )
    latents, queries, keys, values = pl.pallas_call(
        project,
        out_shape=(
            jax.ShapeDtypeStruct((1, 2, 2, 256), F32),
            jax.ShapeDtypeStruct((128, 256), BF16),
            jax.ShapeDtypeStruct((128, 256), BF16),
            jax.ShapeDtypeStruct((128, 256), BF16),
        ),
        in_specs=[vmem] * 5,
        out_specs=(vmem,) * 4,
    )(*travelled)
    merged = (N, 2, 1, 8, 2 * HD)
    return (
        latents,
        queries.reshape(merged),
        keys.reshape(merged),
        values.reshape(merged),
    )


def solution(mesh):
    placed = (
        P("dp", "tm", "height", None, None),
        P(("tm", "height"), "dp"),
        P("dp"),
        P("dp"),
        P(None, "dp", None),
        P(),
        P(),
        P(),
        P(("tm", "height"), "dp"),
        P("dp"),
        P(),
        P(),
        P("tm"),
        P("height"),
    )
    return jax.shard_map(
        shards,
        mesh=mesh,
        in_specs=placed,
        out_specs=(
            P("dp", "tm", "height", None),
            P(None, "tm", "height", None, "dp"),
            P(None, "tm", "height", None, "dp"),
            P(None, "tm", "height", None, "dp"),
        ),
        check_vma=False,
    )
```

```python
import math

import jax
import jax.numpy as jnp
from jax import lax
from jax.experimental import pallas as pl
from jax.experimental.pallas import tpu as pltpu
from jax.sharding import PartitionSpec as P

HD = 128
GROUPS = 32
TAPS = 27
N = 8

norm_eps = 1e-06
latent_scale = 0.476986
rope_base = 256.0
time_dims = 16
row_dims = 56

F32 = jnp.float32
BF16 = jnp.bfloat16
MESH = pl.DeviceIdType.MESH

SLOT_STEP = (0, -1, 1, -2, 2, -3, 3, -4)

ROW = (2, 0, 1, 3)

NT = (((1,), (1,)), ((), ()))


def iota(shape, dim):
    return lax.broadcasted_iota(jnp.int32, shape, dim)


def part_of(ref, which):
    return ref.at[pl.ds(0, 2), pl.ds(2 * which, 2)]


def kernel(
    x_ref,
    wi_ref,
    gg_ref,
    gb_ref,
    wo_ref,
    ob_ref,
    pw_ref,
    pb_ref,
    qw_ref,
    qb_ref,
    qg_ref,
    kg_ref,
    fp_ref,
    rp_ref,
    lat_ref,
    pat_ref,
    wcc_ref,
    bias_ref,
    trig_ref,
    xe,
    nx,
    nr,
    wi,
    gg,
    gb,
    wo,
    ob,
    pw,
    pbias,
    qw,
    qb,
    qg,
    kg,
    wg,
    bt,
    ht,
    w2,
    place,
    wp,
    wr,
    wsum,
    wrh,
    wth,
    wf,
    st,
    outs,
    rz,
    ext,
    rh,
    pb,
    in_sem,
    zr_s,
    zr_r,
    zl_s,
    zl_r,
    ha_s,
    ha_r,
    nx_s,
    nx_r,
    wy_s,
    wy_r,
    wx_s,
    wx_r,
    co_s,
    co_r,
    wc_s,
    wc_r,
    ss_s,
    ss_r,
    rz_s,
    rz_r,
    rh_s,
    rh_r,
    pb_s,
    pb_r,
):
    z = lax.axis_index("dp")
    tm = lax.axis_index("tm")
    hh = lax.axis_index("height")
    core = lax.rem(tm, 2)
    y_lo = tm // 2
    x = hh // 2
    y_hi = lax.rem(hh, 2)
    y = y_hi * 4 + y_lo

    def at_y(where):
        return (z, lax.rem(where, 4) * 2 + core, x * 2 + where // 4)

    def remote(src, dst, send, recv, device):
        return pltpu.make_async_remote_copy(
            src_ref=src,
            dst_ref=dst,
            send_sem=send,
            recv_sem=recv,
            device_id=device,
            device_id_type=MESH,
        )

    sent = []

    def go(copy):
        copy.start()
        sent.append(copy.wait_send)

    def go_if(condition, make):
        pl.when(condition)(lambda: make().start())
        sent.append(lambda: pl.when(condition)(lambda: make().wait_send()))

    def each(fn, end=N):
        def body(k, _):
            fn(k)
            return 0

        lax.fori_loop(1, end, body, 0)

    def go_each(make, end=N):
        each(lambda k: make(k).start(), end)
        sent.append(lambda: each(lambda k: make(k).wait_send(), end))

    def finish(keep=0):
        while len(sent) > keep:
            sent.pop(0)()

    z_up = (lax.rem(z + 1, N), tm, hh)
    z_down = (lax.rem(z + N - 1, N), tm, hh)
    other_core = (z, tm + 1 - 2 * core, hh)

    barrier = pltpu.get_barrier_semaphore()

    def greet(device):
        pl.semaphore_signal(barrier, inc=1, device_id=device, device_id_type=MESH)

    def in_plane(k):
        return (z, lax.rem(tm + k // N, N), lax.rem(hh + lax.rem(k, N), N))

    each(lambda k: greet((lax.rem(z + k, N), tm, hh)))
    each(lambda k: greet(in_plane(k)), N * N)

    d = tm * N + hh
    tile = jnp.minimum(48 * d // 128, 22)
    shift = 48 * d - 128 * tile
    window = pl.ds(pl.multiple_of(tile * 128, 128), 256)
    own = xe.at[0]
    staged = [
        (wi_ref, wi),
        (x_ref, part_of(own, 0)),
        (pw_ref.at[:, window], pw),
        (pb_ref, pbias),
        (qw_ref, qw),
        (wo_ref, wo),
        (gg_ref, gg),
        (gb_ref, gb),
        (ob_ref, ob),
        (qb_ref, qb),
        (qg_ref, qg),
        (kg_ref, kg),
    ]
    staged = [
        pltpu.make_async_copy(src, dst, in_sem.at[i]) for i, (src, dst) in enumerate(staged)
    ]
    for copy in staged:
        copy.start()

    wg[y, core, x] = jnp.zeros((64, 256), BF16)
    staged[0].wait()
    wg[y, core, x, :, pl.ds(0, 216)] = wi[...]
    staged[1].wait()

    pl.semaphore_wait(barrier, N - 1 + N * N - 1)

    def z_right(step, part):
        return remote(
            part_of(xe.at[SLOT_STEP.index(1 - step)], part),
            part_of(xe.at[SLOT_STEP.index(-step)], part),
            zr_s.at[step - 1, part],
            zr_r.at[step - 1, part],
            z_up,
        )

    def z_left(step, part):
        return remote(
            part_of(xe.at[SLOT_STEP.index(step - 1)], part),
            part_of(xe.at[SLOT_STEP.index(step)], part),
            zl_s.at[step - 1, part],
            zl_r.at[step - 1, part],
            z_down,
        )

    def z_first(part):
        go(z_right(1, part))
        go(z_left(1, part))

    has_next = tm < N - 1
    has_last = tm > 0
    has_up = hh < N - 1
    has_down = hh > 0
    next_tm = lax.rem(tm + 1, N)
    up_h = lax.rem(hh + 1, N)
    down_h = lax.rem(hh + N - 1, N)
    halos = (
        (own.at[:, pl.ds(0, 1)], own.at[:, pl.ds(3, 1)], (z, tm, down_h), has_down, has_up),
        (own.at[:, pl.ds(1, 1)], own.at[:, pl.ds(2, 1)], (z, tm, up_h), has_up, has_down),
    )

    def halo_copy(i):
        src, dst, device, _, _ = halos[i]
        return remote(src, dst, ha_s.at[i], ha_r.at[i], device)

    def halo_wait(i):
        pl.when(halos[i][4])(lambda: halo_copy(i).wait_recv())

    for i in range(2):
        go_if(halos[i][3], lambda i=i: halo_copy(i))
    z_first(0)

    def y_copy(k, source):
        return remote(
            wg.at[y, core, x],
            wg.at[source, core, x],
            wy_s.at[k],
            wy_r.at[k],
            at_y(lax.rem(y + k, N)),
        )

    def x_copy(k, i, source):
        line = lax.rem(y + N - k, N)
        return remote(
            wg.at[line, core, x],
            wg.at[line, core, source],
            wx_s.at[k, i],
            wx_r.at[k, i],
            (z, tm, lax.rem(hh + 2 * i, N)),
        )

    def core_copy(k, source):
        line = lax.rem(y + N - k, N)
        return remote(
            wg.at[line, core], wg.at[line, source], co_s.at[k], co_r.at[k], other_core
        )

    y_order = (1, 7, 2, 6, 3, 5, 4)
    for k in y_order:
        go(y_copy(k, y))
    for i in (1, 3, 2):
        go(x_copy(0, i, x))

    for copy in staged[2:5]:
        copy.wait()
    bias_rows = pbias[...].astype(F32)
    bias_tile = iota((24, 128), 0)
    bias_row = jnp.concatenate(
        [
            jnp.sum(jnp.where(bias_tile == tile + i, bias_rows, 0.0), axis=0, keepdims=True)
            for i in range(2)
        ],
        axis=1,
    )
    embed = jnp.concatenate([pw[...].astype(F32), jnp.broadcast_to(bias_row, (8, 256))], axis=0)
    embed = pltpu.roll(embed, lax.rem(256 - shift, 256), 1)[:, :48].astype(BF16)
    part = jnp.dot(embed, qw[...], preferred_element_type=F32)
    for row in range(9):
        for lane in range(6):
            wp[row * 6 + lane] = part[8 * row : 8 * row + 8, 128 * lane : 128 * lane + 128]
    wp[pl.ds(54, 10)] = jnp.zeros((10, 8, 128), F32)

    def fold_1(k):
        to = lax.rem(tm + k, N)
        return remote(
            wp.at[pl.ds(8 * to, 8)], wr.at[k], wc_s.at[0, k], wc_r.at[0, k], (z, to, hh)
        )

    def fold_2(k):
        to = lax.rem(hh + k, N)
        return remote(wsum.at[to], wrh.at[k], wc_s.at[1, k], wc_r.at[1, k], (z, tm, to))

    def fold_3(k, source):
        to = lax.rem(hh + k, N)
        return remote(
            wth.at[hh], wth.at[source], wc_s.at[2, k], wc_r.at[2, k], (z, tm, to)
        )

    def fold_4(k, source):
        to = lax.rem(tm + k, N)
        return remote(
            wf.at[tm], wf.at[source], wc_s.at[3, k], wc_r.at[3, k], (z, to, hh)
        )

    def ring_part(step, part):
        z_right(step, part).wait_recv()
        if step < 4:
            go(z_right(step + 1, part))
            z_left(step, part).wait_recv()
        if step < 3:
            go(z_left(step + 1, part))

    ring_part(1, 0)
    halo_wait(0)
    halo_wait(1)

    @pl.when(jnp.logical_not(has_down))
    def _():
        xe[0, :, 2:3] = xe[0, :, 0:1]

    @pl.when(jnp.logical_not(has_up))
    def _():
        xe[0, :, 3:4] = xe[0, :, 1:2]

    z_first(1)
    ring_part(2, 0)
    for k in y_order:
        y_copy(k, lax.rem(y + N - k, N)).wait_recv()
        for i in (1, 3, 2):
            go(x_copy(k, i, x))

    ring_part(1, 1)
    go_each(lambda k: fold_1(k))
    ring_part(3, 0)
    ring_part(2, 1)

    for k in (0,) + y_order:
        for i in range(1, 4):
            x_copy(k, i, lax.rem(x + 4 - i, 4)).wait_recv()
        go(core_copy(k, core))

    ring_part(3, 1)

    each(lambda k: fold_1(k).wait_recv())
    total = wp[pl.ds(8 * tm, 8)]
    for k in range(1, N):
        total = total + wr[k]
    wsum[...] = total
    go_each(lambda k: fold_2(k))

    for k in range(N):
        core_copy(k, 1 - core).wait_recv()

    def shard_of(index):
        t, h = index // N, index % N
        return wg[(h % 2) * 4 + t // 2, t % 2, h // 2]

    for tile in range(4 * TAPS):
        source, first = (128 * tile) // 216, (128 * tile) % 216
        count = min(128, 216 - first)
        value = shard_of(source)[:, first : first + count]
        if count < 128:
            value = jnp.concatenate([value, shard_of(source + 1)[:, : 128 - count]], axis=1)
        tap = tile // 4
        ij, l = tap // 3, tap % 3
        at = 128 * (tile % 4)
        bt[ij, 64 * l : 64 * l + 64, at : at + 128] = value

    col = iota((64, 128), 1) & 15

    late = ((iota((64, 128), 1) >> 5) & 1) == 1

    def next_copy(pair):
        return remote(
            nx.at[pair], nr.at[pair], nx_s.at[pair], nx_r.at[pair], (z, next_tm, hh)
        )

    def conv_pair(pair):
        by_frame = [jnp.zeros((192, 128), F32) for _ in range(3)]
        for j in range(3):
            rows = [xe[2 * pair : 2 * pair + 2, :, ROW[j + r]] for r in range(2)]
            block = jnp.stack(rows, axis=2).reshape(128, 512)
            for i in range(3):
                by_frame[i] = by_frame[i] + lax.dot_general(
                    bt[3 * i + j], block, NT, preferred_element_type=F32
                )
        moved = []
        for total in by_frame:
            left, mid, right = total[:64], total[64:128], total[128:]
            left = jnp.where(col == 0, left, pltpu.roll(left, 1, 1))
            right = jnp.where(col == 15, right, pltpu.roll(right, 127, 1))
            moved.append(left + mid + right)
        two_on, one_on, same = moved
        ht[pair] = same + jnp.where(late, pltpu.roll(one_on, 32, 1), 0.0)
        nx[pair] = two_on + jnp.where(late, 0.0, pltpu.roll(one_on, 96, 1))
        go_if(has_next, lambda: next_copy(pair))

        @pl.when(jnp.logical_not(has_last))
        def _():
            nr[pair] = jnp.where(late, pltpu.roll(two_on, 32, 1), two_on + one_on)

    for pair in range(3):
        conv_pair(pair)
    for part in range(2):
        ring_part(4, part)
    conv_pair(3)

    stat_lane = iota((8, 128), 1)
    compact = jnp.zeros((8, 128), F32)
    for pair in range(4):
        pl.when(has_last)(lambda pair=pair: next_copy(pair).wait_recv())
        value = ht[pair] + nr[pair]
        ht[pair] = value
        sums = jnp.sum(value.reshape(4, 16, 128), axis=1)
        squares = jnp.sum((value * value).reshape(4, 16, 128), axis=1)
        both = jnp.concatenate([sums, squares], axis=0)
        low = jnp.sum(jnp.where(stat_lane < 64, both, 0.0), axis=1, keepdims=True)
        high = jnp.sum(jnp.where(stat_lane >= 64, both, 0.0), axis=1, keepdims=True)
        compact = jnp.where(stat_lane == pair, low, compact)
        compact = jnp.where(stat_lane == 64 + pair, high, compact)
    st[0:1] = jnp.sum(pltpu.roll(compact, 0, 1, stride=4, stride_axis=0), axis=0, keepdims=True)

    def stat_copy(k):
        return remote(st.at[pl.ds(0, 1)], st.at[pl.ds(k, 1)], ss_s, ss_r, in_plane(k))

    each(lambda k: stat_copy(k).start(), N * N)
    others = st.at[pl.ds(1, N * N - 1)]
    finish()

    for copy in staged[5:]:
        copy.wait()
    for ij in range(9):
        w2[16 * ij : 16 * ij + 16] = jnp.concatenate(
            [wo[3 * ij + l].astype(F32) for l in range(3)], axis=1
        ).astype(BF16)

    lane = iota((128, 512), 1)
    row = iota((128, 512), 0)
    s_at = (lane >> 6) & 3
    q_at = (lane >> 4) & 3
    f_at = (row >> 5) & 1
    r_at = (row >> 4) & 1
    in_frame = (s_at == f_at + 2) | ((tm == 0) & (s_at < 2) & (f_at == 0))
    in_row = (
        (q_at == r_at + 1)
        | ((hh == 0) & (q_at == 0) & (r_at == 0))
        | ((hh == N - 1) & (q_at == 3) & (r_at == 1))
    )
    same = ((lane & 15) == (row & 15)) & ((lane >> 8) == (row >> 6))
    place[...] = jnp.where(in_frame & in_row & same, 1.0, 0.0).astype(BF16)

    each(lambda k: fold_2(k).wait_recv())
    tile_sum = wsum[hh]
    for k in range(1, N):
        tile_sum = tile_sum + wrh[k]
    wth[hh] = tile_sum
    go_each(lambda k: fold_3(k, hh))

    diag = iota((64, 64), 0) == iota((64, 64), 1)
    gain = jnp.sum(jnp.where(diag, gg[...].astype(F32), 0.0), axis=1, keepdims=True)
    bias = jnp.sum(jnp.where(diag, gb[...].astype(F32), 0.0), axis=1, keepdims=True)
    diag = iota((16, 16), 0) == iota((16, 16), 1)
    out_bias = jnp.sum(jnp.where(diag, ob[...], 0.0), axis=1, keepdims=True)

    remote(others, others, ss_s, ss_r, in_plane(1)).wait()
    total = jnp.broadcast_to(jnp.sum(st[...], axis=0, keepdims=True), (8, 128))
    compact = pltpu.roll(total, 100, 1, stride=4, stride_axis=0)
    count = float(16 * 16 * 16 * 16)
    average = compact / count
    mean = average
    var = pltpu.roll(average, 4, 0) - mean * mean
    inv = lax.rsqrt(var + norm_eps)

    wide = iota((16, 512), 1)
    t_at = (wide >> 6) & 3
    u_at = (wide >> 4) & 3
    lane_128 = iota((8, 128), 1)

    def spread(value, pair):
        lanes = jnp.where(
            lane_128 < 64,
            jnp.broadcast_to(value[:, pair : pair + 1], (8, 128)),
            jnp.broadcast_to(value[:, 64 + pair : 65 + pair], (8, 128)),
        )
        return jnp.concatenate(
            [jnp.broadcast_to(lanes[7 - g : 8 - g], (16, 128)) for g in range(4)], axis=0
        )

    def rz_copy(slot):
        to = lax.rem(z + N + SLOT_STEP[slot], N)
        return remote(outs.at[slot], rz.at[slot], rz_s.at[slot], rz_r.at[slot], (to, tm, hh))

    for pair in (3, 2, 1, 0):
        scale = spread(inv, pair) * gain
        offset = bias - spread(mean, pair) * scale
        value = ht[pair] * scale + offset
        value = value / (1.0 + jnp.exp(-value))
        left = jnp.where(col == 0, value, pltpu.roll(value, 1, 1))
        right = jnp.where(col == 15, value, pltpu.roll(value, 127, 1))
        stacked = jnp.concatenate([left, value, right], axis=0).astype(BF16)
        spots = jnp.dot(stacked, place[...], preferred_element_type=F32).astype(BF16)
        taps = jnp.dot(w2[...], spots, preferred_element_type=F32)
        total = jnp.zeros((16, 512), F32)
        for ij in range(9):
            i, j = ij // 3, ij % 3
            move = (16 * (1 - j) - 64 * i) % 512
            moved = taps[16 * ij : 16 * ij + 16]
            if move:
                moved = pltpu.roll(moved, move, 1)
            valid = t_at <= 3 - i
            if j == 0:
                valid = valid & (u_at >= 1)
            if j == 2:
                valid = valid & (u_at <= 2)
            total = total + jnp.where(valid, moved, 0.0)
        outs[2 * pair] = total[:, :256]
        outs[2 * pair + 1] = total[:, 256:]
        for slot in (2 * pair + 1, 2 * pair):
            if slot:
                go(rz_copy(slot))

    goes = (
        has_next,
        has_down,
        has_up,
        has_next & has_down,
        has_next & has_up,
    )
    comes = (
        has_last,
        has_up,
        has_down,
        has_last & has_up,
        has_last & has_down,
    )
    for i in range(5):

        @pl.when(jnp.logical_not(comes[i]))
        def _(i=i):
            rh[i] = jnp.zeros((16, 128), F32)

    each(lambda k: fold_3(k, lax.rem(hh + N - k, N)).wait_recv())
    wf[tm] = wth[...]
    go_each(lambda k: fold_4(k, tm))

    finish(7)

    entry = iota((16, 128), 1) >> 1
    token = iota((16, 128), 0)
    is_frame = entry < 8
    is_row = entry < 36
    start = jnp.where(is_frame, 0, jnp.where(is_row, 8, 36))
    width = jnp.where(is_frame, float(time_dims), float(row_dims))
    power = 2.0 * (entry - start).astype(F32) / width
    freq = jnp.exp(power * (-math.log(rope_base)))
    frame_at = jnp.where(token < 8, fp_ref[0].astype(F32), fp_ref[1].astype(F32))
    spot = jnp.where(
        is_frame,
        frame_at,
        jnp.where(is_row, rp_ref[0].astype(F32), (token & 7).astype(F32)),
    )
    angle = spot * freq
    odd = (iota((16, 128), 1) & 1) == 1
    cosine = jnp.cos(angle)
    sine = jnp.sin(angle)
    sine = jnp.where(odd, sine, -sine)
    for i, gain_of in enumerate((qg, kg)):
        gain_row = jnp.broadcast_to(gain_of[...].astype(F32), (16, 128))
        swapped = jnp.where(odd, pltpu.roll(gain_row, 1, 1), pltpu.roll(gain_row, 127, 1))
        trig_ref[2 * i] = cosine * gain_row
        trig_ref[2 * i + 1] = sine * swapped

    total = outs[0]
    for slot in range(1, N):
        rz_copy(slot).wait_recv()
        total = total + rz[slot]
    ext[0] = total[:, :128]
    ext[1] = total[:, 128:]

    def rh_copy(i):
        return remote(
            ext.at[1 if i in (0, 3, 4) else 0],
            rh.at[i],
            rh_s.at[i],
            rh_r.at[i],
            (
                (z, next_tm, hh),
                (z, tm, down_h),
                (z, tm, up_h),
                (z, next_tm, down_h),
                (z, next_tm, up_h),
            )[i],
        )

    for i in range(5):
        go_if(goes[i], lambda i=i: rh_copy(i))
    for i in range(5):
        pl.when(comes[i])(lambda i=i: rh_copy(i).wait_recv())

    narrow = iota((16, 128), 1)
    u_at = (narrow >> 4) & 3
    inside = (u_at == 1) | (u_at == 2)
    latent = jnp.where(inside, total[:, :128] + rh[0], 0.0)
    latent = latent + jnp.where(u_at == 2, pltpu.roll(rh[1] + rh[3], 32, 1), 0.0)
    latent = latent + jnp.where(u_at == 1, pltpu.roll(rh[2] + rh[4], 96, 1), 0.0)
    latent = (latent + out_bias) * latent_scale

    lane = iota((128, 128), 1)
    group = (iota((128, 128), 0) >> 4) & 3
    keep = (((lane >> 4) & 3) == (group >> 1) + 1) & ((lane & 1) == (group & 1))
    rounded = latent.astype(BF16).astype(F32)
    many = jnp.where(keep, jnp.concatenate([rounded] * 8, axis=0), 0.0).astype(BF16)
    lane = iota((16, 128), 1)
    row = iota((16, 128), 0)
    pick = ((lane >> 6) == (row >> 3)) & (((lane & 15) >> 1) == (row & 7))
    pick = jnp.where(pick, 1.0, 0.0).astype(BF16)
    pb[z] = lax.dot_general(pick, many, NT, preferred_element_type=F32).astype(BF16)

    def pb_copy(k, source):
        return remote(
            pb.at[z],
            pb.at[source],
            pb_s.at[k],
            pb_r.at[k],
            (lax.rem(z + k, N), tm, hh),
        )

    go_each(lambda k: pb_copy(k, z))
    finish(1)

    each(lambda k: fold_4(k, lax.rem(tm + N - k, N)).wait_recv())
    for lane_tile in range(6):
        for pair in range(4):
            tiles = [12 * pair + lane_tile, 12 * pair + 6 + lane_tile]
            value = jnp.concatenate([wf[t // 8, t % 8] for t in tiles], axis=0)
            high = value.astype(BF16)
            low = (value - high.astype(F32)).astype(BF16)
            at = slice(128 * lane_tile, 128 * lane_tile + 128)
            wcc_ref[16 * pair : 16 * pair + 16, at] = high
            wcc_ref[64 + 16 * pair : 64 + 16 * pair + 16, at] = low
    proj_bias = qb[...].astype(F32)
    bias_ref[...] = jnp.concatenate(
        [
            wf[6 + lane_tile // 8, lane_tile % 8][0:1] + proj_bias[lane_tile : lane_tile + 1]
            for lane_tile in range(6)
        ],
        axis=1,
    )

    lane = iota((256, 128), 1)
    row = iota((256, 128), 0)
    many = jnp.where((lane & 15) == (row >> 4), jnp.concatenate([latent] * 16, axis=0), 0.0)
    lane = iota((8, 128), 1)
    row = iota((8, 128), 0)
    pick = ((lane >> 6) == (row >> 1)) & (((lane >> 4) & 3) == (row & 1) + 1)
    pick = jnp.where(pick, 1.0, 0.0)
    lines = lax.dot_general(
        pick, many, NT, preferred_element_type=F32, precision=lax.Precision.HIGHEST
    )
    lat_ref[...] = lines[:4]

    each(lambda k: pb_copy(k, lax.rem(z + N - k, N)).wait_recv())
    pat_ref[...] = pb[...].reshape(128, 128)

    finish()


def project(lat_in, pat_ref, wcc_ref, bias_ref, trig_ref, lat_ref, q_ref, k_ref, v_ref):
    for row in range(4):
        lat_ref[0, row // 2, row % 2 : row % 2 + 1] = lat_in[row : row + 1]
    odd = (iota((128, 128), 1) & 1) == 1
    projected = jnp.dot(pat_ref[...], wcc_ref[...], preferred_element_type=F32)
    projected = projected + bias_ref[...]

    def turned(value, which):
        cosine = jnp.concatenate([trig_ref[2 * which]] * 8, axis=0)
        sine = jnp.concatenate([trig_ref[2 * which + 1]] * 8, axis=0)
        mean_square = jnp.mean(value * value, axis=1, keepdims=True)
        value = value * lax.rsqrt(mean_square + norm_eps)
        swapped = jnp.where(odd, pltpu.roll(value, 1, 1), pltpu.roll(value, 127, 1))
        return (value * cosine + swapped * sine).astype(BF16)

    for head in range(2):
        at = slice(HD * head, HD * head + HD)
        base = 3 * HD * head
        q_ref[:, at] = turned(projected[:, base : base + HD], 0)
        k_ref[:, at] = turned(projected[:, base + HD : base + 2 * HD], 1)
        v_ref[:, at] = projected[:, base + 2 * HD : base + 3 * HD].astype(BF16)


def shards(
    clip_inputs,
    conv_in_weight,
    group_gain,
    group_bias,
    conv_out_weight,
    out_bias,
    patch_weight,
    patch_bias,
    qkv_weight,
    qkv_bias,
    q_gain,
    k_gain,
    frame_pos,
    row_pos,
):
    vmem = pl.BlockSpec(memory_space=pltpu.VMEM)
    smem = pl.BlockSpec(memory_space=pltpu.SMEM)
    hbm = pl.BlockSpec(memory_space=pltpu.HBM)
    dma = pltpu.SemaphoreType.DMA
    travelled = pl.pallas_call(
        kernel,
        out_shape=(
            jax.ShapeDtypeStruct((4, 256), F32),
            jax.ShapeDtypeStruct((128, 128), BF16),
            jax.ShapeDtypeStruct((128, 768), BF16),
            jax.ShapeDtypeStruct((1, 768), F32),
            jax.ShapeDtypeStruct((4, 16, 128), F32),
        ),
        in_specs=[hbm] * 12 + [smem] * 2,
        out_specs=(vmem,) * 5,
        scratch_shapes=[
            pltpu.VMEM((N, 2, 4, 16, 512), BF16),
            pltpu.VMEM((4, 64, 128), F32),
            pltpu.VMEM((4, 64, 128), F32),
            pltpu.VMEM((64, 216), BF16),
            pltpu.VMEM((1, 64), BF16),
            pltpu.VMEM((1, 64), BF16),
            pltpu.VMEM((TAPS, 16, 64), BF16),
            pltpu.VMEM((1, 16), F32),
            pltpu.VMEM((64, 256), BF16),
            pltpu.VMEM((24, 128), BF16),
            pltpu.VMEM((48, 768), BF16),
            pltpu.VMEM((6, 128), BF16),
            pltpu.VMEM((1, 128), BF16),
            pltpu.VMEM((1, 128), BF16),
            pltpu.VMEM((N, 2, 4, 64, 256), BF16),
            pltpu.VMEM((9, 192, 512), BF16),
            pltpu.VMEM((4, 64, 128), F32),
            pltpu.VMEM((144, 192), BF16),
            pltpu.VMEM((128, 512), BF16),
            pltpu.VMEM((64, 8, 128), F32),
            pltpu.VMEM((N, 8, 8, 128), F32),
            pltpu.VMEM((8, 8, 128), F32),
            pltpu.VMEM((N, 8, 128), F32),
            pltpu.VMEM((N, 8, 128), F32),
            pltpu.VMEM((N, 8, 8, 128), F32),
            pltpu.VMEM((N * N, 128), F32),
            pltpu.VMEM((N, 16, 256), F32),
            pltpu.VMEM((N, 16, 256), F32),
            pltpu.VMEM((2, 16, 128), F32),
            pltpu.VMEM((5, 16, 128), F32),
            pltpu.VMEM((N, 16, 128), BF16),
            dma((12,)),
            dma((4, 2)),
            dma((4, 2)),
            dma((3, 2)),
            dma((3, 2)),
            dma((2,)),
            dma((2,)),
            dma((4,)),
            dma((4,)),
            dma((N,)),
            dma((N,)),
            dma((N, 4)),
            dma((N, 4)),
            dma((N,)),
            dma((N,)),
            dma((4, N)),
            dma((4, N)),
            dma,
            dma,
            dma((N,)),
            dma((N,)),
            dma((5,)),
            dma((5,)),
            dma((N,)),
            dma((N,)),
        ],
        compiler_params=pltpu.CompilerParams(
            collective_id=0, has_side_effects=True, vmem_limit_bytes=63 * 2**20
        ),
    )(
        clip_inputs[0],
        conv_in_weight.T,
        group_gain[None],
        group_bias[None],
        conv_out_weight.transpose(0, 2, 1),
        out_bias[None],
        patch_weight,
        patch_bias.reshape(24, 128),
        qkv_weight,
        qkv_bias.reshape(6, 128),
        q_gain[None],
        k_gain[None],
        frame_pos,
        row_pos,
    )
    latents, queries, keys, values = pl.pallas_call(
        project,
        out_shape=(
            jax.ShapeDtypeStruct((1, 2, 2, 256), F32),
            jax.ShapeDtypeStruct((128, 256), BF16),
            jax.ShapeDtypeStruct((128, 256), BF16),
            jax.ShapeDtypeStruct((128, 256), BF16),
        ),
        in_specs=[vmem] * 5,
        out_specs=(vmem,) * 4,
    )(*travelled)
    merged = (N, 2, 1, 8, 2 * HD)
    return (
        latents,
        queries.reshape(merged),
        keys.reshape(merged),
        values.reshape(merged),
    )


def solution(mesh):
    placed = (
        P("dp", "tm", "height", None, None),
        P(("tm", "height"), "dp"),
        P("dp"),
        P("dp"),
        P(None, "dp", None),
        P(),
        P(),
        P(),
        P(("tm", "height"), "dp"),
        P("dp"),
        P(),
        P(),
        P("tm"),
        P("height"),
    )
    return jax.shard_map(
        shards,
        mesh=mesh,
        in_specs=placed,
        out_specs=(
            P("dp", "tm", "height", None),
            P(None, "tm", "height", None, "dp"),
            P(None, "tm", "height", None, "dp"),
            P(None, "tm", "height", None, "dp"),
        ),
        check_vma=False,
    )
```

```python
import math

import jax
import jax.numpy as jnp
from jax import lax
from jax.experimental import pallas as pl
from jax.experimental.pallas import tpu as pltpu
from jax.sharding import PartitionSpec as P

HD = 128
GROUPS = 32
TAPS = 27
N = 8

norm_eps = 1e-06
latent_scale = 0.476986
rope_base = 256.0
time_dims = 16
row_dims = 56

F32 = jnp.float32
BF16 = jnp.bfloat16
MESH = pl.DeviceIdType.MESH

SLOT_STEP = (0, -1, 1, -2, 2, -3, 3, -4)

ROW = (2, 0, 1, 3)

NT = (((1,), (1,)), ((), ()))


def iota(shape, dim):
    return lax.broadcasted_iota(jnp.int32, shape, dim)


def part_of(ref, which):
    return ref.at[pl.ds(0, 2), pl.ds(2 * which, 2)]


def kernel(
    x_ref,
    wi_ref,
    gg_ref,
    gb_ref,
    wo_ref,
    ob_ref,
    pw_ref,
    pb_ref,
    qw_ref,
    qb_ref,
    qg_ref,
    kg_ref,
    fp_ref,
    rp_ref,
    lat_ref,
    pat_ref,
    wcc_ref,
    bias_ref,
    trig_ref,
    xe,
    nx,
    nr,
    wi,
    gg,
    gb,
    wo,
    ob,
    pw,
    pbias,
    qw,
    qb,
    qg,
    kg,
    wg,
    bt,
    ht,
    w2,
    place,
    wp,
    wr,
    wsum,
    wrh,
    wth,
    wf,
    st,
    outs,
    rz,
    ext,
    rh,
    pb,
    in_sem,
    zr_s,
    zr_r,
    zl_s,
    zl_r,
    ha_s,
    ha_r,
    nx_s,
    nx_r,
    wy_s,
    wy_r,
    wx_s,
    wx_r,
    co_s,
    co_r,
    wc_s,
    wc_r,
    ss_s,
    ss_r,
    rz_s,
    rz_r,
    rh_s,
    rh_r,
    pb_s,
    pb_r,
):
    z = lax.axis_index("dp")
    tm = lax.axis_index("tm")
    hh = lax.axis_index("height")
    core = lax.rem(tm, 2)
    y_lo = tm // 2
    x = hh // 2
    y_hi = lax.rem(hh, 2)
    y = y_hi * 4 + y_lo

    def at_y(where):
        return (z, lax.rem(where, 4) * 2 + core, x * 2 + where // 4)

    def remote(src, dst, send, recv, device):
        return pltpu.make_async_remote_copy(
            src_ref=src,
            dst_ref=dst,
            send_sem=send,
            recv_sem=recv,
            device_id=device,
            device_id_type=MESH,
        )

    sent = []

    def go(copy):
        copy.start()
        sent.append(copy.wait_send)

    def go_if(condition, make):
        pl.when(condition)(lambda: make().start())
        sent.append(lambda: pl.when(condition)(lambda: make().wait_send()))

    def each(fn, end=N):
        def body(k, _):
            fn(k)
            return 0

        lax.fori_loop(1, end, body, 0)

    def go_each(make, end=N):
        each(lambda k: make(k).start(), end)
        sent.append(lambda: each(lambda k: make(k).wait_send(), end))

    def finish(keep=0):
        while len(sent) > keep:
            sent.pop(0)()

    z_up = (lax.rem(z + 1, N), tm, hh)
    z_down = (lax.rem(z + N - 1, N), tm, hh)
    other_core = (z, tm + 1 - 2 * core, hh)

    d = tm * N + hh
    tile = jnp.minimum(48 * d // 128, 22)
    shift = 48 * d - 128 * tile
    window = pl.ds(pl.multiple_of(tile * 128, 128), 256)
    own = xe.at[0]
    staged = [
        (x_ref, part_of(own, 0)),
        (wi_ref, wi),
        (pw_ref.at[:, window], pw),
        (pb_ref, pbias),
        (qw_ref, qw),
        (wo_ref, wo),
        (gg_ref, gg),
        (gb_ref, gb),
        (ob_ref, ob),
        (qb_ref, qb),
        (qg_ref, qg),
        (kg_ref, kg),
    ]
    staged = [
        pltpu.make_async_copy(src, dst, in_sem.at[i]) for i, (src, dst) in enumerate(staged)
    ]
    for copy in staged:
        copy.start()

    barrier = pltpu.get_barrier_semaphore()

    def greet(device):
        pl.semaphore_signal(barrier, inc=1, device_id=device, device_id_type=MESH)

    def in_plane(k):
        return (z, lax.rem(tm + k // N, N), lax.rem(hh + lax.rem(k, N), N))

    each(lambda k: greet((lax.rem(z + k, N), tm, hh)))
    each(lambda k: greet(in_plane(k)), N * N)

    staged[0].wait()
    pl.semaphore_wait(barrier, N - 1 + N * N - 1)

    def z_right(step, part):
        return remote(
            part_of(xe.at[SLOT_STEP.index(1 - step)], part),
            part_of(xe.at[SLOT_STEP.index(-step)], part),
            zr_s.at[step - 1, part],
            zr_r.at[step - 1, part],
            z_up,
        )

    def z_left(step, part):
        return remote(
            part_of(xe.at[SLOT_STEP.index(step - 1)], part),
            part_of(xe.at[SLOT_STEP.index(step)], part),
            zl_s.at[step - 1, part],
            zl_r.at[step - 1, part],
            z_down,
        )

    def z_first(part):
        go(z_right(1, part))
        go(z_left(1, part))

    has_next = tm < N - 1
    has_last = tm > 0
    has_up = hh < N - 1
    has_down = hh > 0
    next_tm = lax.rem(tm + 1, N)
    up_h = lax.rem(hh + 1, N)
    down_h = lax.rem(hh + N - 1, N)
    halos = (
        (own.at[:, pl.ds(0, 1)], own.at[:, pl.ds(3, 1)], (z, tm, down_h), has_down, has_up),
        (own.at[:, pl.ds(1, 1)], own.at[:, pl.ds(2, 1)], (z, tm, up_h), has_up, has_down),
    )

    def halo_copy(i):
        src, dst, device, _, _ = halos[i]
        return remote(src, dst, ha_s.at[i], ha_r.at[i], device)

    def halo_wait(i):
        pl.when(halos[i][4])(lambda: halo_copy(i).wait_recv())

    for i in range(2):
        go_if(halos[i][3], lambda i=i: halo_copy(i))
    z_first(0)

    wg[y, core, x] = jnp.zeros((64, 256), BF16)
    staged[1].wait()
    wg[y, core, x, :, pl.ds(0, 216)] = wi[...]

    def y_copy(k, source):
        return remote(
            wg.at[y, core, x],
            wg.at[source, core, x],
            wy_s.at[k],
            wy_r.at[k],
            at_y(lax.rem(y + k, N)),
        )

    def x_copy(k, i, source):
        line = lax.rem(y + N - k, N)
        return remote(
            wg.at[line, core, x],
            wg.at[line, core, source],
            wx_s.at[k, i],
            wx_r.at[k, i],
            (z, tm, lax.rem(hh + 2 * i, N)),
        )

    def core_copy(k, source):
        line = lax.rem(y + N - k, N)
        return remote(
            wg.at[line, core], wg.at[line, source], co_s.at[k], co_r.at[k], other_core
        )

    y_order = (1, 7, 2, 6, 3, 5, 4)

    def along_x(order):
        for k in order:
            y_copy(k, lax.rem(y + N - k, N)).wait_recv()
            for i in (1, 3, 2):
                go(x_copy(k, i, x))


    for copy in staged[2:5]:
        copy.wait()
    bias_rows = pbias[...].astype(F32)
    bias_tile = iota((24, 128), 0)
    bias_row = jnp.concatenate(
        [
            jnp.sum(jnp.where(bias_tile == tile + i, bias_rows, 0.0), axis=0, keepdims=True)
            for i in range(2)
        ],
        axis=1,
    )
    embed = jnp.concatenate([pw[...].astype(F32), jnp.broadcast_to(bias_row, (8, 256))], axis=0)
    embed = pltpu.roll(embed, lax.rem(256 - shift, 256), 1)[:, :48].astype(BF16)
    part = jnp.dot(embed, qw[...], preferred_element_type=F32)
    for row in range(9):
        for lane in range(6):
            wp[row * 6 + lane] = part[8 * row : 8 * row + 8, 128 * lane : 128 * lane + 128]
    wp[pl.ds(54, 10)] = jnp.zeros((10, 8, 128), F32)

    for k in y_order:
        go(y_copy(k, y))
    for i in (1, 3, 2):
        go(x_copy(0, i, x))

    def fold_1(k):
        to = lax.rem(tm + k, N)
        return remote(
            wp.at[pl.ds(8 * to, 8)], wr.at[k], wc_s.at[0, k], wc_r.at[0, k], (z, to, hh)
        )

    def fold_2(k):
        to = lax.rem(hh + k, N)
        return remote(wsum.at[to], wrh.at[k], wc_s.at[1, k], wc_r.at[1, k], (z, tm, to))

    def fold_3(k, source):
        to = lax.rem(hh + k, N)
        return remote(
            wth.at[hh], wth.at[source], wc_s.at[2, k], wc_r.at[2, k], (z, tm, to)
        )

    def fold_4(k, source):
        to = lax.rem(tm + k, N)
        return remote(
            wf.at[tm], wf.at[source], wc_s.at[3, k], wc_r.at[3, k], (z, to, hh)
        )

    def ring_part(step, part):
        z_right(step, part).wait_recv()
        if step < 4:
            go(z_right(step + 1, part))
            z_left(step, part).wait_recv()
        if step < 3:
            go(z_left(step + 1, part))

    ring_part(1, 0)
    halo_wait(0)
    halo_wait(1)

    @pl.when(jnp.logical_not(has_down))
    def _():
        xe[0, :, 2:3] = xe[0, :, 0:1]

    @pl.when(jnp.logical_not(has_up))
    def _():
        xe[0, :, 3:4] = xe[0, :, 1:2]

    z_first(1)
    along_x(y_order)
    ring_part(2, 0)
    ring_part(1, 1)
    go_each(lambda k: fold_1(k))
    ring_part(3, 0)
    ring_part(2, 1)

    for k in (0,) + y_order:
        for i in range(1, 4):
            x_copy(k, i, lax.rem(x + 4 - i, 4)).wait_recv()
        go(core_copy(k, core))

    ring_part(3, 1)

    each(lambda k: fold_1(k).wait_recv())
    total = wp[pl.ds(8 * tm, 8)]
    for k in range(1, N):
        total = total + wr[k]
    wsum[...] = total
    go_each(lambda k: fold_2(k))

    for k in range(N):
        core_copy(k, 1 - core).wait_recv()

    def shard_of(index):
        t, h = index // N, index % N
        return wg[(h % 2) * 4 + t // 2, t % 2, h // 2]

    for tile in range(4 * TAPS):
        source, first = (128 * tile) // 216, (128 * tile) % 216
        count = min(128, 216 - first)
        value = shard_of(source)[:, first : first + count]
        if count < 128:
            value = jnp.concatenate([value, shard_of(source + 1)[:, : 128 - count]], axis=1)
        tap = tile // 4
        ij, l = tap // 3, tap % 3
        at = 128 * (tile % 4)
        bt[ij, 64 * l : 64 * l + 64, at : at + 128] = value

    col = iota((64, 128), 1) & 15

    late = ((iota((64, 128), 1) >> 5) & 1) == 1

    def next_copy(pair):
        return remote(
            nx.at[pair], nr.at[pair], nx_s.at[pair], nx_r.at[pair], (z, next_tm, hh)
        )

    def conv_pair(pair):
        by_frame = [jnp.zeros((192, 128), F32) for _ in range(3)]
        for j in range(3):
            rows = [xe[2 * pair : 2 * pair + 2, :, ROW[j + r]] for r in range(2)]
            block = jnp.stack(rows, axis=2).reshape(128, 512)
            for i in range(3):
                by_frame[i] = by_frame[i] + lax.dot_general(
                    bt[3 * i + j], block, NT, preferred_element_type=F32
                )
        moved = []
        for total in by_frame:
            left, mid, right = total[:64], total[64:128], total[128:]
            left = jnp.where(col == 0, left, pltpu.roll(left, 1, 1))
            right = jnp.where(col == 15, right, pltpu.roll(right, 127, 1))
            moved.append(left + mid + right)
        two_on, one_on, same = moved
        ht[pair] = same + jnp.where(late, pltpu.roll(one_on, 32, 1), 0.0)
        nx[pair] = two_on + jnp.where(late, 0.0, pltpu.roll(one_on, 96, 1))
        go_if(has_next, lambda: next_copy(pair))

        @pl.when(jnp.logical_not(has_last))
        def _():
            nr[pair] = jnp.where(late, pltpu.roll(two_on, 32, 1), two_on + one_on)

    for pair in range(3):
        conv_pair(pair)
    for part in range(2):
        ring_part(4, part)
    conv_pair(3)

    stat_lane = iota((8, 128), 1)
    compact = jnp.zeros((8, 128), F32)
    for pair in range(4):
        pl.when(has_last)(lambda pair=pair: next_copy(pair).wait_recv())
        value = ht[pair] + nr[pair]
        ht[pair] = value
        sums = jnp.sum(value.reshape(4, 16, 128), axis=1)
        squares = jnp.sum((value * value).reshape(4, 16, 128), axis=1)
        both = jnp.concatenate([sums, squares], axis=0)
        low = jnp.sum(jnp.where(stat_lane < 64, both, 0.0), axis=1, keepdims=True)
        high = jnp.sum(jnp.where(stat_lane >= 64, both, 0.0), axis=1, keepdims=True)
        compact = jnp.where(stat_lane == pair, low, compact)
        compact = jnp.where(stat_lane == 64 + pair, high, compact)
    st[0:1] = jnp.sum(pltpu.roll(compact, 0, 1, stride=4, stride_axis=0), axis=0, keepdims=True)

    def stat_copy(k):
        return remote(st.at[pl.ds(0, 1)], st.at[pl.ds(k, 1)], ss_s, ss_r, in_plane(k))

    each(lambda k: stat_copy(k).start(), N * N)
    others = st.at[pl.ds(1, N * N - 1)]
    finish()

    for copy in staged[5:]:
        copy.wait()
    for ij in range(9):
        w2[16 * ij : 16 * ij + 16] = jnp.concatenate(
            [wo[3 * ij + l].astype(F32) for l in range(3)], axis=1
        ).astype(BF16)

    lane = iota((128, 512), 1)
    row = iota((128, 512), 0)
    s_at = (lane >> 6) & 3
    q_at = (lane >> 4) & 3
    f_at = (row >> 5) & 1
    r_at = (row >> 4) & 1
    in_frame = (s_at == f_at + 2) | ((tm == 0) & (s_at < 2) & (f_at == 0))
    in_row = (
        (q_at == r_at + 1)
        | ((hh == 0) & (q_at == 0) & (r_at == 0))
        | ((hh == N - 1) & (q_at == 3) & (r_at == 1))
    )
    same = ((lane & 15) == (row & 15)) & ((lane >> 8) == (row >> 6))
    place[...] = jnp.where(in_frame & in_row & same, 1.0, 0.0).astype(BF16)

    each(lambda k: fold_2(k).wait_recv())
    tile_sum = wsum[hh]
    for k in range(1, N):
        tile_sum = tile_sum + wrh[k]
    wth[hh] = tile_sum
    go_each(lambda k: fold_3(k, hh))

    diag = iota((64, 64), 0) == iota((64, 64), 1)
    gain = jnp.sum(jnp.where(diag, gg[...].astype(F32), 0.0), axis=1, keepdims=True)
    bias = jnp.sum(jnp.where(diag, gb[...].astype(F32), 0.0), axis=1, keepdims=True)
    diag = iota((16, 16), 0) == iota((16, 16), 1)
    out_bias = jnp.sum(jnp.where(diag, ob[...], 0.0), axis=1, keepdims=True)

    remote(others, others, ss_s, ss_r, in_plane(1)).wait()
    total = jnp.broadcast_to(jnp.sum(st[...], axis=0, keepdims=True), (8, 128))
    compact = pltpu.roll(total, 100, 1, stride=4, stride_axis=0)
    count = float(16 * 16 * 16 * 16)
    average = compact / count
    mean = average
    var = pltpu.roll(average, 4, 0) - mean * mean
    inv = lax.rsqrt(var + norm_eps)

    wide = iota((16, 512), 1)
    t_at = (wide >> 6) & 3
    u_at = (wide >> 4) & 3
    lane_128 = iota((8, 128), 1)

    def spread(value, pair):
        lanes = jnp.where(
            lane_128 < 64,
            jnp.broadcast_to(value[:, pair : pair + 1], (8, 128)),
            jnp.broadcast_to(value[:, 64 + pair : 65 + pair], (8, 128)),
        )
        return jnp.concatenate(
            [jnp.broadcast_to(lanes[7 - g : 8 - g], (16, 128)) for g in range(4)], axis=0
        )

    def rz_copy(slot):
        to = lax.rem(z + N + SLOT_STEP[slot], N)
        return remote(outs.at[slot], rz.at[slot], rz_s.at[slot], rz_r.at[slot], (to, tm, hh))

    for pair in (3, 2, 1, 0):
        scale = spread(inv, pair) * gain
        offset = bias - spread(mean, pair) * scale
        value = ht[pair] * scale + offset
        value = value / (1.0 + jnp.exp(-value))
        left = jnp.where(col == 0, value, pltpu.roll(value, 1, 1))
        right = jnp.where(col == 15, value, pltpu.roll(value, 127, 1))
        stacked = jnp.concatenate([left, value, right], axis=0).astype(BF16)
        spots = jnp.dot(stacked, place[...], preferred_element_type=F32).astype(BF16)
        taps = jnp.dot(w2[...], spots, preferred_element_type=F32)
        total = jnp.zeros((16, 512), F32)
        for ij in range(9):
            i, j = ij // 3, ij % 3
            move = (16 * (1 - j) - 64 * i) % 512
            moved = taps[16 * ij : 16 * ij + 16]
            if move:
                moved = pltpu.roll(moved, move, 1)
            valid = t_at <= 3 - i
            if j == 0:
                valid = valid & (u_at >= 1)
            if j == 2:
                valid = valid & (u_at <= 2)
            total = total + jnp.where(valid, moved, 0.0)
        outs[2 * pair] = total[:, :256]
        outs[2 * pair + 1] = total[:, 256:]
        for slot in (2 * pair + 1, 2 * pair):
            if slot:
                go(rz_copy(slot))

    goes = (
        has_next,
        has_down,
        has_up,
        has_next & has_down,
        has_next & has_up,
    )
    comes = (
        has_last,
        has_up,
        has_down,
        has_last & has_up,
        has_last & has_down,
    )
    for i in range(5):

        @pl.when(jnp.logical_not(comes[i]))
        def _(i=i):
            rh[i] = jnp.zeros((16, 128), F32)

    each(lambda k: fold_3(k, lax.rem(hh + N - k, N)).wait_recv())
    wf[tm] = wth[...]
    go_each(lambda k: fold_4(k, tm))

    finish(7)

    entry = iota((16, 128), 1) >> 1
    token = iota((16, 128), 0)
    is_frame = entry < 8
    is_row = entry < 36
    start = jnp.where(is_frame, 0, jnp.where(is_row, 8, 36))
    width = jnp.where(is_frame, float(time_dims), float(row_dims))
    power = 2.0 * (entry - start).astype(F32) / width
    freq = jnp.exp(power * (-math.log(rope_base)))
    frame_at = jnp.where(token < 8, fp_ref[0].astype(F32), fp_ref[1].astype(F32))
    spot = jnp.where(
        is_frame,
        frame_at,
        jnp.where(is_row, rp_ref[0].astype(F32), (token & 7).astype(F32)),
    )
    angle = spot * freq
    odd = (iota((16, 128), 1) & 1) == 1
    cosine = jnp.cos(angle)
    sine = jnp.sin(angle)
    sine = jnp.where(odd, sine, -sine)
    for i, gain_of in enumerate((qg, kg)):
        gain_row = jnp.broadcast_to(gain_of[...].astype(F32), (16, 128))
        swapped = jnp.where(odd, pltpu.roll(gain_row, 1, 1), pltpu.roll(gain_row, 127, 1))
        trig_ref[2 * i] = cosine * gain_row
        trig_ref[2 * i + 1] = sine * swapped

    total = outs[0]
    for slot in range(1, N):
        rz_copy(slot).wait_recv()
        total = total + rz[slot]
    ext[0] = total[:, :128]
    ext[1] = total[:, 128:]

    def rh_copy(i):
        return remote(
            ext.at[1 if i in (0, 3, 4) else 0],
            rh.at[i],
            rh_s.at[i],
            rh_r.at[i],
            (
                (z, next_tm, hh),
                (z, tm, down_h),
                (z, tm, up_h),
                (z, next_tm, down_h),
                (z, next_tm, up_h),
            )[i],
        )

    for i in range(5):
        go_if(goes[i], lambda i=i: rh_copy(i))
    for i in range(5):
        pl.when(comes[i])(lambda i=i: rh_copy(i).wait_recv())

    narrow = iota((16, 128), 1)
    u_at = (narrow >> 4) & 3
    inside = (u_at == 1) | (u_at == 2)
    latent = jnp.where(inside, total[:, :128] + rh[0], 0.0)
    latent = latent + jnp.where(u_at == 2, pltpu.roll(rh[1] + rh[3], 32, 1), 0.0)
    latent = latent + jnp.where(u_at == 1, pltpu.roll(rh[2] + rh[4], 96, 1), 0.0)
    latent = (latent + out_bias) * latent_scale

    lane = iota((128, 128), 1)
    group = (iota((128, 128), 0) >> 4) & 3
    keep = (((lane >> 4) & 3) == (group >> 1) + 1) & ((lane & 1) == (group & 1))
    rounded = latent.astype(BF16).astype(F32)
    many = jnp.where(keep, jnp.concatenate([rounded] * 8, axis=0), 0.0).astype(BF16)
    lane = iota((16, 128), 1)
    row = iota((16, 128), 0)
    pick = ((lane >> 6) == (row >> 3)) & (((lane & 15) >> 1) == (row & 7))
    pick = jnp.where(pick, 1.0, 0.0).astype(BF16)
    pb[z] = lax.dot_general(pick, many, NT, preferred_element_type=F32).astype(BF16)

    def pb_copy(k, source):
        return remote(
            pb.at[z],
            pb.at[source],
            pb_s.at[k],
            pb_r.at[k],
            (lax.rem(z + k, N), tm, hh),
        )

    go_each(lambda k: pb_copy(k, z))
    finish(1)

    each(lambda k: fold_4(k, lax.rem(tm + N - k, N)).wait_recv())
    for lane_tile in range(6):
        for pair in range(4):
            tiles = [12 * pair + lane_tile, 12 * pair + 6 + lane_tile]
            value = jnp.concatenate([wf[t // 8, t % 8] for t in tiles], axis=0)
            high = value.astype(BF16)
            low = (value - high.astype(F32)).astype(BF16)
            at = slice(128 * lane_tile, 128 * lane_tile + 128)
            wcc_ref[16 * pair : 16 * pair + 16, at] = high
            wcc_ref[64 + 16 * pair : 64 + 16 * pair + 16, at] = low
    proj_bias = qb[...].astype(F32)
    bias_ref[...] = jnp.concatenate(
        [
            wf[6 + lane_tile // 8, lane_tile % 8][0:1] + proj_bias[lane_tile : lane_tile + 1]
            for lane_tile in range(6)
        ],
        axis=1,
    )

    lane = iota((256, 128), 1)
    row = iota((256, 128), 0)
    many = jnp.where((lane & 15) == (row >> 4), jnp.concatenate([latent] * 16, axis=0), 0.0)
    lane = iota((8, 128), 1)
    row = iota((8, 128), 0)
    pick = ((lane >> 6) == (row >> 1)) & (((lane >> 4) & 3) == (row & 1) + 1)
    pick = jnp.where(pick, 1.0, 0.0)
    lines = lax.dot_general(
        pick, many, NT, preferred_element_type=F32, precision=lax.Precision.HIGHEST
    )
    lat_ref[...] = lines[:4]

    each(lambda k: pb_copy(k, lax.rem(z + N - k, N)).wait_recv())
    pat_ref[...] = pb[...].reshape(128, 128)

    finish()


def project(lat_in, pat_ref, wcc_ref, bias_ref, trig_ref, lat_ref, q_ref, k_ref, v_ref):
    for row in range(4):
        lat_ref[0, row // 2, row % 2 : row % 2 + 1] = lat_in[row : row + 1]
    odd = (iota((128, 128), 1) & 1) == 1
    projected = jnp.dot(pat_ref[...], wcc_ref[...], preferred_element_type=F32)
    projected = projected + bias_ref[...]

    def turned(value, which):
        cosine = jnp.concatenate([trig_ref[2 * which]] * 8, axis=0)
        sine = jnp.concatenate([trig_ref[2 * which + 1]] * 8, axis=0)
        mean_square = jnp.mean(value * value, axis=1, keepdims=True)
        value = value * lax.rsqrt(mean_square + norm_eps)
        swapped = jnp.where(odd, pltpu.roll(value, 1, 1), pltpu.roll(value, 127, 1))
        return (value * cosine + swapped * sine).astype(BF16)

    for head in range(2):
        at = slice(HD * head, HD * head + HD)
        base = 3 * HD * head
        q_ref[:, at] = turned(projected[:, base : base + HD], 0)
        k_ref[:, at] = turned(projected[:, base + HD : base + 2 * HD], 1)
        v_ref[:, at] = projected[:, base + 2 * HD : base + 3 * HD].astype(BF16)


def shards(
    clip_inputs,
    conv_in_weight,
    group_gain,
    group_bias,
    conv_out_weight,
    out_bias,
    patch_weight,
    patch_bias,
    qkv_weight,
    qkv_bias,
    q_gain,
    k_gain,
    frame_pos,
    row_pos,
):
    vmem = pl.BlockSpec(memory_space=pltpu.VMEM)
    smem = pl.BlockSpec(memory_space=pltpu.SMEM)
    hbm = pl.BlockSpec(memory_space=pltpu.HBM)
    dma = pltpu.SemaphoreType.DMA
    travelled = pl.pallas_call(
        kernel,
        out_shape=(
            jax.ShapeDtypeStruct((4, 256), F32),
            jax.ShapeDtypeStruct((128, 128), BF16),
            jax.ShapeDtypeStruct((128, 768), BF16),
            jax.ShapeDtypeStruct((1, 768), F32),
            jax.ShapeDtypeStruct((4, 16, 128), F32),
        ),
        in_specs=[hbm] * 12 + [smem] * 2,
        out_specs=(vmem,) * 5,
        scratch_shapes=[
            pltpu.VMEM((N, 2, 4, 16, 512), BF16),
            pltpu.VMEM((4, 64, 128), F32),
            pltpu.VMEM((4, 64, 128), F32),
            pltpu.VMEM((64, 216), BF16),
            pltpu.VMEM((1, 64), BF16),
            pltpu.VMEM((1, 64), BF16),
            pltpu.VMEM((TAPS, 16, 64), BF16),
            pltpu.VMEM((1, 16), F32),
            pltpu.VMEM((64, 256), BF16),
            pltpu.VMEM((24, 128), BF16),
            pltpu.VMEM((48, 768), BF16),
            pltpu.VMEM((6, 128), BF16),
            pltpu.VMEM((1, 128), BF16),
            pltpu.VMEM((1, 128), BF16),
            pltpu.VMEM((N, 2, 4, 64, 256), BF16),
            pltpu.VMEM((9, 192, 512), BF16),
            pltpu.VMEM((4, 64, 128), F32),
            pltpu.VMEM((144, 192), BF16),
            pltpu.VMEM((128, 512), BF16),
            pltpu.VMEM((64, 8, 128), F32),
            pltpu.VMEM((N, 8, 8, 128), F32),
            pltpu.VMEM((8, 8, 128), F32),
            pltpu.VMEM((N, 8, 128), F32),
            pltpu.VMEM((N, 8, 128), F32),
            pltpu.VMEM((N, 8, 8, 128), F32),
            pltpu.VMEM((N * N, 128), F32),
            pltpu.VMEM((N, 16, 256), F32),
            pltpu.VMEM((N, 16, 256), F32),
            pltpu.VMEM((2, 16, 128), F32),
            pltpu.VMEM((5, 16, 128), F32),
            pltpu.VMEM((N, 16, 128), BF16),
            dma((12,)),
            dma((4, 2)),
            dma((4, 2)),
            dma((3, 2)),
            dma((3, 2)),
            dma((2,)),
            dma((2,)),
            dma((4,)),
            dma((4,)),
            dma((N,)),
            dma((N,)),
            dma((N, 4)),
            dma((N, 4)),
            dma((N,)),
            dma((N,)),
            dma((4, N)),
            dma((4, N)),
            dma,
            dma,
            dma((N,)),
            dma((N,)),
            dma((5,)),
            dma((5,)),
            dma((N,)),
            dma((N,)),
        ],
        compiler_params=pltpu.CompilerParams(
            collective_id=0, has_side_effects=True, vmem_limit_bytes=63 * 2**20
        ),
    )(
        clip_inputs[0],
        conv_in_weight.T,
        group_gain[None],
        group_bias[None],
        conv_out_weight.transpose(0, 2, 1),
        out_bias[None],
        patch_weight,
        patch_bias.reshape(24, 128),
        qkv_weight,
        qkv_bias.reshape(6, 128),
        q_gain[None],
        k_gain[None],
        frame_pos,
        row_pos,
    )
    latents, queries, keys, values = pl.pallas_call(
        project,
        out_shape=(
            jax.ShapeDtypeStruct((1, 2, 2, 256), F32),
            jax.ShapeDtypeStruct((128, 256), BF16),
            jax.ShapeDtypeStruct((128, 256), BF16),
            jax.ShapeDtypeStruct((128, 256), BF16),
        ),
        in_specs=[vmem] * 5,
        out_specs=(vmem,) * 4,
    )(*travelled)
    merged = (N, 2, 1, 8, 2 * HD)
    return (
        latents,
        queries.reshape(merged),
        keys.reshape(merged),
        values.reshape(merged),
    )


def solution(mesh):
    placed = (
        P("dp", "tm", "height", None, None),
        P(("tm", "height"), "dp"),
        P("dp"),
        P("dp"),
        P(None, "dp", None),
        P(),
        P(),
        P(),
        P(("tm", "height"), "dp"),
        P("dp"),
        P(),
        P(),
        P("tm"),
        P("height"),
    )
    return jax.shard_map(
        shards,
        mesh=mesh,
        in_specs=placed,
        out_specs=(
            P("dp", "tm", "height", None),
            P(None, "tm", "height", None, "dp"),
            P(None, "tm", "height", None, "dp"),
            P(None, "tm", "height", None, "dp"),
        ),
        check_vma=False,
    )
```

```python
import math

import jax
import jax.numpy as jnp
from jax import lax
from jax.experimental import pallas as pl
from jax.experimental.pallas import tpu as pltpu
from jax.sharding import PartitionSpec as P

HD = 128
GROUPS = 32
TAPS = 27
N = 8

norm_eps = 1e-06
latent_scale = 0.476986
rope_base = 256.0
time_dims = 16
row_dims = 56

F32 = jnp.float32
BF16 = jnp.bfloat16
MESH = pl.DeviceIdType.MESH

SLOT_STEP = (0, -1, 1, -2, 2, -3, 3, -4)

ROW = (2, 0, 1, 3)

NT = (((1,), (1,)), ((), ()))


def iota(shape, dim):
    return lax.broadcasted_iota(jnp.int32, shape, dim)


def part_of(ref, which):
    return ref.at[pl.ds(0, 2), pl.ds(2 * which, 2)]


def kernel(
    x_ref,
    wi_ref,
    gg_ref,
    gb_ref,
    wo_ref,
    ob_ref,
    pw_ref,
    pb_ref,
    qw_ref,
    qb_ref,
    qg_ref,
    kg_ref,
    fp_ref,
    rp_ref,
    lat_ref,
    pat_ref,
    wcc_ref,
    bias_ref,
    trig_ref,
    xe,
    nx,
    nr,
    wi,
    gg,
    gb,
    wo,
    ob,
    pw,
    pbias,
    qw,
    qb,
    qg,
    kg,
    wg,
    bt,
    ht,
    w2,
    place,
    wp,
    wr,
    wsum,
    wrh,
    wth,
    wf,
    st,
    outs,
    rz,
    ext,
    rh,
    pb,
    in_sem,
    zr_s,
    zr_r,
    zl_s,
    zl_r,
    ha_s,
    ha_r,
    nx_s,
    nx_r,
    wy_s,
    wy_r,
    wx_s,
    wx_r,
    co_s,
    co_r,
    wc_s,
    wc_r,
    ss_s,
    ss_r,
    rz_s,
    rz_r,
    rh_s,
    rh_r,
    pb_s,
    pb_r,
):
    z = lax.axis_index("dp")
    tm = lax.axis_index("tm")
    hh = lax.axis_index("height")
    core = lax.rem(tm, 2)
    y_lo = tm // 2
    x = hh // 2
    y_hi = lax.rem(hh, 2)
    y = y_hi * 4 + y_lo

    def at_y(where):
        return (z, lax.rem(where, 4) * 2 + core, x * 2 + where // 4)

    def remote(src, dst, send, recv, device):
        return pltpu.make_async_remote_copy(
            src_ref=src,
            dst_ref=dst,
            send_sem=send,
            recv_sem=recv,
            device_id=device,
            device_id_type=MESH,
        )

    sent = []

    def go(copy):
        copy.start()
        sent.append(copy.wait_send)

    def go_if(condition, make):
        pl.when(condition)(lambda: make().start())
        sent.append(lambda: pl.when(condition)(lambda: make().wait_send()))

    def each(fn, end=N):
        def body(k, _):
            fn(k)
            return 0

        lax.fori_loop(1, end, body, 0)

    def go_each(make, end=N):
        each(lambda k: make(k).start(), end)
        sent.append(lambda: each(lambda k: make(k).wait_send(), end))

    def finish(keep=0):
        while len(sent) > keep:
            sent.pop(0)()

    z_up = (lax.rem(z + 1, N), tm, hh)
    z_down = (lax.rem(z + N - 1, N), tm, hh)
    other_core = (z, tm + 1 - 2 * core, hh)

    d = tm * N + hh
    tile = jnp.minimum(48 * d // 128, 22)
    shift = 48 * d - 128 * tile
    window = pl.ds(pl.multiple_of(tile * 128, 128), 256)
    own = xe.at[0]
    staged = [
        (x_ref, part_of(own, 0)),
        (wi_ref, wi),
        (pw_ref.at[:, window], pw),
        (pb_ref, pbias),
        (qw_ref, qw),
        (wo_ref, wo),
        (gg_ref, gg),
        (gb_ref, gb),
        (ob_ref, ob),
        (qb_ref, qb),
        (qg_ref, qg),
        (kg_ref, kg),
    ]
    staged = [
        pltpu.make_async_copy(src, dst, in_sem.at[i]) for i, (src, dst) in enumerate(staged)
    ]
    for copy in staged:
        copy.start()

    barrier = pltpu.get_barrier_semaphore()

    def greet(device):
        pl.semaphore_signal(barrier, inc=1, device_id=device, device_id_type=MESH)

    def in_plane(k):
        return (z, lax.rem(tm + k // N, N), lax.rem(hh + lax.rem(k, N), N))

    each(lambda k: greet((lax.rem(z + k, N), tm, hh)))
    each(lambda k: greet(in_plane(k)), N * N)

    staged[0].wait()
    pl.semaphore_wait(barrier, N - 1 + N * N - 1)

    def z_right(step, part):
        return remote(
            part_of(xe.at[SLOT_STEP.index(1 - step)], part),
            part_of(xe.at[SLOT_STEP.index(-step)], part),
            zr_s.at[step - 1, part],
            zr_r.at[step - 1, part],
            z_up,
        )

    def z_left(step, part):
        return remote(
            part_of(xe.at[SLOT_STEP.index(step - 1)], part),
            part_of(xe.at[SLOT_STEP.index(step)], part),
            zl_s.at[step - 1, part],
            zl_r.at[step - 1, part],
            z_down,
        )

    def z_first(part):
        go(z_right(1, part))
        go(z_left(1, part))

    has_next = tm < N - 1
    has_last = tm > 0
    has_up = hh < N - 1
    has_down = hh > 0
    next_tm = lax.rem(tm + 1, N)
    up_h = lax.rem(hh + 1, N)
    down_h = lax.rem(hh + N - 1, N)
    halos = (
        (own.at[:, pl.ds(0, 1)], own.at[:, pl.ds(3, 1)], (z, tm, down_h), has_down, has_up),
        (own.at[:, pl.ds(1, 1)], own.at[:, pl.ds(2, 1)], (z, tm, up_h), has_up, has_down),
    )

    def halo_copy(i):
        src, dst, device, _, _ = halos[i]
        return remote(src, dst, ha_s.at[i], ha_r.at[i], device)

    def halo_wait(i):
        pl.when(halos[i][4])(lambda: halo_copy(i).wait_recv())

    for i in range(2):
        go_if(halos[i][3], lambda i=i: halo_copy(i))
    z_first(0)

    wg[y, core, x] = jnp.zeros((64, 256), BF16)
    staged[1].wait()
    wg[y, core, x, :, pl.ds(0, 216)] = wi[...]

    def y_copy(k, source):
        return remote(
            wg.at[y, core, x],
            wg.at[source, core, x],
            wy_s.at[k],
            wy_r.at[k],
            at_y(lax.rem(y + k, N)),
        )

    def x_copy(k, i, source):
        line = lax.rem(y + N - k, N)
        return remote(
            wg.at[line, core, x],
            wg.at[line, core, source],
            wx_s.at[k, i],
            wx_r.at[k, i],
            (z, tm, lax.rem(hh + 2 * i, N)),
        )

    def core_copy(k, source):
        line = lax.rem(y + N - k, N)
        return remote(
            wg.at[line, core], wg.at[line, source], co_s.at[k], co_r.at[k], other_core
        )

    y_order = (1, 7, 2, 6, 3, 5, 4)

    def along_x(order):
        for k in order:
            y_copy(k, lax.rem(y + N - k, N)).wait_recv()
            for i in (1, 3, 2):
                go(x_copy(k, i, x))


    for copy in staged[2:5]:
        copy.wait()
    bias_rows = pbias[...].astype(F32)
    bias_tile = iota((24, 128), 0)
    bias_row = jnp.concatenate(
        [
            jnp.sum(jnp.where(bias_tile == tile + i, bias_rows, 0.0), axis=0, keepdims=True)
            for i in range(2)
        ],
        axis=1,
    )
    embed = jnp.concatenate([pw[...].astype(F32), jnp.broadcast_to(bias_row, (8, 256))], axis=0)
    embed = pltpu.roll(embed, lax.rem(256 - shift, 256), 1)[:, :48].astype(BF16)
    part = jnp.dot(embed, qw[...], preferred_element_type=F32)
    for row in range(9):
        for lane in range(6):
            wp[row * 6 + lane] = part[8 * row : 8 * row + 8, 128 * lane : 128 * lane + 128]
    wp[pl.ds(54, 10)] = jnp.zeros((10, 8, 128), F32)

    for k in y_order:
        go(y_copy(k, y))
    for i in (1, 3, 2):
        go(x_copy(0, i, x))

    def fold_1(k):
        to = lax.rem(tm + k, N)
        return remote(
            wp.at[pl.ds(8 * to, 8)], wr.at[k], wc_s.at[0, k], wc_r.at[0, k], (z, to, hh)
        )

    def fold_2(k):
        to = lax.rem(hh + k, N)
        return remote(wsum.at[to], wrh.at[k], wc_s.at[1, k], wc_r.at[1, k], (z, tm, to))

    def fold_3(k, source):
        to = lax.rem(hh + k, N)
        return remote(
            wth.at[hh], wth.at[source], wc_s.at[2, k], wc_r.at[2, k], (z, tm, to)
        )

    def fold_4(k, source):
        to = lax.rem(tm + k, N)
        return remote(
            wf.at[tm], wf.at[source], wc_s.at[3, k], wc_r.at[3, k], (z, to, hh)
        )

    def ring_part(step, part):
        z_right(step, part).wait_recv()
        if step < 4:
            go(z_right(step + 1, part))
            z_left(step, part).wait_recv()
        if step < 3:
            go(z_left(step + 1, part))

    ring_part(1, 0)
    halo_wait(0)
    halo_wait(1)

    @pl.when(jnp.logical_not(has_down))
    def _():
        xe[0, :, 2:3] = xe[0, :, 0:1]

    @pl.when(jnp.logical_not(has_up))
    def _():
        xe[0, :, 3:4] = xe[0, :, 1:2]

    z_first(1)
    along_x(y_order)
    ring_part(2, 0)
    ring_part(1, 1)
    go_each(lambda k: fold_1(k))
    ring_part(3, 0)
    ring_part(2, 1)

    for k in (0,) + y_order:
        for i in range(1, 4):
            x_copy(k, i, lax.rem(x + 4 - i, 4)).wait_recv()
        go(core_copy(k, core))

    ring_part(3, 1)

    each(lambda k: fold_1(k).wait_recv())
    total = wp[pl.ds(8 * tm, 8)]
    for k in range(1, N):
        total = total + wr[k]
    wsum[...] = total
    go_each(lambda k: fold_2(k))

    for k in range(N):
        core_copy(k, 1 - core).wait_recv()

    def shard_of(index):
        t, h = index // N, index % N
        return wg[(h % 2) * 4 + t // 2, t % 2, h // 2]

    for tile in range(4 * TAPS):
        source, first = (128 * tile) // 216, (128 * tile) % 216
        count = min(128, 216 - first)
        value = shard_of(source)[:, first : first + count]
        if count < 128:
            value = jnp.concatenate([value, shard_of(source + 1)[:, : 128 - count]], axis=1)
        tap = tile // 4
        ij, l = tap // 3, tap % 3
        at = 128 * (tile % 4)
        bt[ij, 64 * l : 64 * l + 64, at : at + 128] = value

    col = iota((64, 128), 1) & 15

    late = ((iota((64, 128), 1) >> 5) & 1) == 1

    def next_copy(pair):
        return remote(
            nx.at[pair], nr.at[pair], nx_s.at[pair], nx_r.at[pair], (z, next_tm, hh)
        )

    def conv_pair(pair):
        by_frame = [jnp.zeros((192, 128), F32) for _ in range(3)]
        for j in range(3):
            rows = [xe[2 * pair : 2 * pair + 2, :, ROW[j + r]] for r in range(2)]
            block = jnp.stack(rows, axis=2).reshape(128, 512)
            for i in range(3):
                by_frame[i] = by_frame[i] + lax.dot_general(
                    bt[3 * i + j], block, NT, preferred_element_type=F32
                )
        moved = []
        for total in by_frame:
            left, mid, right = total[:64], total[64:128], total[128:]
            left = jnp.where(col == 0, left, pltpu.roll(left, 1, 1))
            right = jnp.where(col == 15, right, pltpu.roll(right, 127, 1))
            moved.append(left + mid + right)
        two_on, one_on, same = moved
        ht[pair] = same + jnp.where(late, pltpu.roll(one_on, 32, 1), 0.0)
        nx[pair] = two_on + jnp.where(late, 0.0, pltpu.roll(one_on, 96, 1))
        go_if(has_next, lambda: next_copy(pair))

        @pl.when(jnp.logical_not(has_last))
        def _():
            nr[pair] = jnp.where(late, pltpu.roll(two_on, 32, 1), two_on + one_on)

    for pair in range(3):
        conv_pair(pair)
    for part in range(2):
        ring_part(4, part)
    conv_pair(3)

    stat_lane = iota((8, 128), 1)
    compact = jnp.zeros((8, 128), F32)
    for pair in range(4):
        pl.when(has_last)(lambda pair=pair: next_copy(pair).wait_recv())
        value = ht[pair] + nr[pair]
        ht[pair] = value
        sums = jnp.sum(value.reshape(4, 16, 128), axis=1)
        squares = jnp.sum((value * value).reshape(4, 16, 128), axis=1)
        both = jnp.concatenate([sums, squares], axis=0)
        low = jnp.sum(jnp.where(stat_lane < 64, both, 0.0), axis=1, keepdims=True)
        high = jnp.sum(jnp.where(stat_lane >= 64, both, 0.0), axis=1, keepdims=True)
        compact = jnp.where(stat_lane == pair, low, compact)
        compact = jnp.where(stat_lane == 64 + pair, high, compact)
    st[0:1] = jnp.sum(pltpu.roll(compact, 0, 1, stride=4, stride_axis=0), axis=0, keepdims=True)

    def stat_copy(k):
        return remote(st.at[pl.ds(0, 1)], st.at[pl.ds(k, 1)], ss_s, ss_r, in_plane(k))

    each(lambda k: stat_copy(k).start(), N * N)
    others = st.at[pl.ds(1, N * N - 1)]
    finish()

    for copy in staged[5:]:
        copy.wait()
    for ij in range(9):
        w2[16 * ij : 16 * ij + 16] = jnp.concatenate(
            [wo[3 * ij + l].astype(F32) for l in range(3)], axis=1
        ).astype(BF16)

    lane = iota((128, 512), 1)
    row = iota((128, 512), 0)
    s_at = (lane >> 6) & 3
    q_at = (lane >> 4) & 3
    f_at = (row >> 5) & 1
    r_at = (row >> 4) & 1
    in_frame = (s_at == f_at + 2) | ((tm == 0) & (s_at < 2) & (f_at == 0))
    in_row = (
        (q_at == r_at + 1)
        | ((hh == 0) & (q_at == 0) & (r_at == 0))
        | ((hh == N - 1) & (q_at == 3) & (r_at == 1))
    )
    same = ((lane & 15) == (row & 15)) & ((lane >> 8) == (row >> 6))
    place[...] = jnp.where(in_frame & in_row & same, 1.0, 0.0).astype(BF16)

    each(lambda k: fold_2(k).wait_recv())
    tile_sum = wsum[hh]
    for k in range(1, N):
        tile_sum = tile_sum + wrh[k]
    wth[hh] = tile_sum
    go_each(lambda k: fold_3(k, hh))

    diag = iota((64, 64), 0) == iota((64, 64), 1)
    gain = jnp.sum(jnp.where(diag, gg[...].astype(F32), 0.0), axis=1, keepdims=True)
    bias = jnp.sum(jnp.where(diag, gb[...].astype(F32), 0.0), axis=1, keepdims=True)
    diag = iota((16, 16), 0) == iota((16, 16), 1)
    out_bias = jnp.sum(jnp.where(diag, ob[...], 0.0), axis=1, keepdims=True)

    remote(others, others, ss_s, ss_r, in_plane(1)).wait()
    total = jnp.broadcast_to(jnp.sum(st[...], axis=0, keepdims=True), (8, 128))
    compact = pltpu.roll(total, 100, 1, stride=4, stride_axis=0)
    count = float(16 * 16 * 16 * 16)
    average = compact / count
    mean = average
    var = pltpu.roll(average, 4, 0) - mean * mean
    inv = lax.rsqrt(var + norm_eps)

    wide = iota((16, 512), 1)
    t_at = (wide >> 6) & 3
    u_at = (wide >> 4) & 3
    lane_128 = iota((8, 128), 1)

    def spread(value, pair):
        lanes = jnp.where(
            lane_128 < 64,
            jnp.broadcast_to(value[:, pair : pair + 1], (8, 128)),
            jnp.broadcast_to(value[:, 64 + pair : 65 + pair], (8, 128)),
        )
        return jnp.concatenate(
            [jnp.broadcast_to(lanes[7 - g : 8 - g], (16, 128)) for g in range(4)], axis=0
        )

    def rz_copy(slot):
        to = lax.rem(z + N + SLOT_STEP[slot], N)
        return remote(outs.at[slot], rz.at[slot], rz_s.at[slot], rz_r.at[slot], (to, tm, hh))

    for pair in (3, 2, 1, 0):
        scale = spread(inv, pair) * gain
        offset = bias - spread(mean, pair) * scale
        value = ht[pair] * scale + offset
        value = value / (1.0 + jnp.exp(-value))
        left = jnp.where(col == 0, value, pltpu.roll(value, 1, 1))
        right = jnp.where(col == 15, value, pltpu.roll(value, 127, 1))
        stacked = jnp.concatenate([left, value, right], axis=0).astype(BF16)
        spots = jnp.dot(stacked, place[...], preferred_element_type=F32).astype(BF16)
        taps = jnp.dot(w2[...], spots, preferred_element_type=F32)
        total = jnp.zeros((16, 512), F32)
        for ij in range(9):
            i, j = ij // 3, ij % 3
            move = (16 * (1 - j) - 64 * i) % 512
            moved = taps[16 * ij : 16 * ij + 16]
            if move:
                moved = pltpu.roll(moved, move, 1)
            valid = t_at <= 3 - i
            if j == 0:
                valid = valid & (u_at >= 1)
            if j == 2:
                valid = valid & (u_at <= 2)
            total = total + jnp.where(valid, moved, 0.0)
        outs[2 * pair] = total[:, :256]
        outs[2 * pair + 1] = total[:, 256:]
        for slot in (2 * pair + 1, 2 * pair):
            if slot:
                go(rz_copy(slot))

    goes = (
        has_next,
        has_down,
        has_up,
        has_next & has_down,
        has_next & has_up,
    )
    comes = (
        has_last,
        has_up,
        has_down,
        has_last & has_up,
        has_last & has_down,
    )
    for i in range(5):

        @pl.when(jnp.logical_not(comes[i]))
        def _(i=i):
            rh[i] = jnp.zeros((16, 128), F32)

    each(lambda k: fold_3(k, lax.rem(hh + N - k, N)).wait_recv())
    wf[tm] = wth[...]
    go_each(lambda k: fold_4(k, tm))

    finish(7)

    entry = iota((16, 128), 1) >> 1
    token = iota((16, 128), 0)
    is_frame = entry < 8
    is_row = entry < 36
    start = jnp.where(is_frame, 0, jnp.where(is_row, 8, 36))
    width = jnp.where(is_frame, float(time_dims), float(row_dims))
    power = 2.0 * (entry - start).astype(F32) / width
    freq = jnp.exp(power * (-math.log(rope_base)))
    frame_at = jnp.where(token < 8, fp_ref[0].astype(F32), fp_ref[1].astype(F32))
    spot = jnp.where(
        is_frame,
        frame_at,
        jnp.where(is_row, rp_ref[0].astype(F32), (token & 7).astype(F32)),
    )
    angle = spot * freq
    odd = (iota((16, 128), 1) & 1) == 1
    cosine = jnp.cos(angle)
    sine = jnp.sin(angle)
    sine = jnp.where(odd, sine, -sine)
    for i, gain_of in enumerate((qg, kg)):
        gain_row = jnp.broadcast_to(gain_of[...].astype(F32), (16, 128))
        swapped = jnp.where(odd, pltpu.roll(gain_row, 1, 1), pltpu.roll(gain_row, 127, 1))
        trig_ref[2 * i] = cosine * gain_row
        trig_ref[2 * i + 1] = sine * swapped

    total = outs[0]
    for slot in range(1, N):
        rz_copy(slot).wait_recv()
        total = total + rz[slot]
    ext[0] = total[:, :128]
    ext[1] = total[:, 128:]

    def rh_copy(i):
        return remote(
            ext.at[1 if i in (0, 3, 4) else 0],
            rh.at[i],
            rh_s.at[i],
            rh_r.at[i],
            (
                (z, next_tm, hh),
                (z, tm, down_h),
                (z, tm, up_h),
                (z, next_tm, down_h),
                (z, next_tm, up_h),
            )[i],
        )

    for i in (3, 4, 1, 2, 0):
        go_if(goes[i], lambda i=i: rh_copy(i))
    for i in range(5):
        pl.when(comes[i])(lambda i=i: rh_copy(i).wait_recv())

    narrow = iota((16, 128), 1)
    u_at = (narrow >> 4) & 3
    inside = (u_at == 1) | (u_at == 2)
    latent = jnp.where(inside, total[:, :128] + rh[0], 0.0)
    latent = latent + jnp.where(u_at == 2, pltpu.roll(rh[1] + rh[3], 32, 1), 0.0)
    latent = latent + jnp.where(u_at == 1, pltpu.roll(rh[2] + rh[4], 96, 1), 0.0)
    latent = (latent + out_bias) * latent_scale

    lane = iota((128, 128), 1)
    group = (iota((128, 128), 0) >> 4) & 3
    keep = (((lane >> 4) & 3) == (group >> 1) + 1) & ((lane & 1) == (group & 1))
    rounded = latent.astype(BF16).astype(F32)
    many = jnp.where(keep, jnp.concatenate([rounded] * 8, axis=0), 0.0).astype(BF16)
    lane = iota((16, 128), 1)
    row = iota((16, 128), 0)
    pick = ((lane >> 6) == (row >> 3)) & (((lane & 15) >> 1) == (row & 7))
    pick = jnp.where(pick, 1.0, 0.0).astype(BF16)
    pb[z] = lax.dot_general(pick, many, NT, preferred_element_type=F32).astype(BF16)

    def pb_copy(k, source):
        return remote(
            pb.at[z],
            pb.at[source],
            pb_s.at[k],
            pb_r.at[k],
            (lax.rem(z + k, N), tm, hh),
        )

    for k in (4, 3, 5, 2, 6, 1, 7):
        go(pb_copy(k, z))
    finish(N - 1)

    each(lambda k: fold_4(k, lax.rem(tm + N - k, N)).wait_recv())
    for lane_tile in range(6):
        for pair in range(4):
            tiles = [12 * pair + lane_tile, 12 * pair + 6 + lane_tile]
            value = jnp.concatenate([wf[t // 8, t % 8] for t in tiles], axis=0)
            high = value.astype(BF16)
            low = (value - high.astype(F32)).astype(BF16)
            at = slice(128 * lane_tile, 128 * lane_tile + 128)
            wcc_ref[16 * pair : 16 * pair + 16, at] = high
            wcc_ref[64 + 16 * pair : 64 + 16 * pair + 16, at] = low
    proj_bias = qb[...].astype(F32)
    bias_ref[...] = jnp.concatenate(
        [
            wf[6 + lane_tile // 8, lane_tile % 8][0:1] + proj_bias[lane_tile : lane_tile + 1]
            for lane_tile in range(6)
        ],
        axis=1,
    )

    lane = iota((256, 128), 1)
    row = iota((256, 128), 0)
    many = jnp.where((lane & 15) == (row >> 4), jnp.concatenate([latent] * 16, axis=0), 0.0)
    lane = iota((8, 128), 1)
    row = iota((8, 128), 0)
    pick = ((lane >> 6) == (row >> 1)) & (((lane >> 4) & 3) == (row & 1) + 1)
    pick = jnp.where(pick, 1.0, 0.0)
    lines = lax.dot_general(
        pick, many, NT, preferred_element_type=F32, precision=lax.Precision.HIGHEST
    )
    lat_ref[...] = lines[:4]

    each(lambda k: pb_copy(k, lax.rem(z + N - k, N)).wait_recv())
    pat_ref[...] = pb[...].reshape(128, 128)

    finish()


def project(lat_in, pat_ref, wcc_ref, bias_ref, trig_ref, lat_ref, q_ref, k_ref, v_ref):
    for row in range(4):
        lat_ref[0, row // 2, row % 2 : row % 2 + 1] = lat_in[row : row + 1]
    odd = (iota((128, 128), 1) & 1) == 1
    projected = jnp.dot(pat_ref[...], wcc_ref[...], preferred_element_type=F32)
    projected = projected + bias_ref[...]

    def turned(value, which):
        cosine = jnp.concatenate([trig_ref[2 * which]] * 8, axis=0)
        sine = jnp.concatenate([trig_ref[2 * which + 1]] * 8, axis=0)
        mean_square = jnp.mean(value * value, axis=1, keepdims=True)
        value = value * lax.rsqrt(mean_square + norm_eps)
        swapped = jnp.where(odd, pltpu.roll(value, 1, 1), pltpu.roll(value, 127, 1))
        return (value * cosine + swapped * sine).astype(BF16)

    for head in range(2):
        at = slice(HD * head, HD * head + HD)
        base = 3 * HD * head
        q_ref[:, at] = turned(projected[:, base : base + HD], 0)
        k_ref[:, at] = turned(projected[:, base + HD : base + 2 * HD], 1)
        v_ref[:, at] = projected[:, base + 2 * HD : base + 3 * HD].astype(BF16)


def shards(
    clip_inputs,
    conv_in_weight,
    group_gain,
    group_bias,
    conv_out_weight,
    out_bias,
    patch_weight,
    patch_bias,
    qkv_weight,
    qkv_bias,
    q_gain,
    k_gain,
    frame_pos,
    row_pos,
):
    vmem = pl.BlockSpec(memory_space=pltpu.VMEM)
    smem = pl.BlockSpec(memory_space=pltpu.SMEM)
    hbm = pl.BlockSpec(memory_space=pltpu.HBM)
    dma = pltpu.SemaphoreType.DMA
    travelled = pl.pallas_call(
        kernel,
        out_shape=(
            jax.ShapeDtypeStruct((4, 256), F32),
            jax.ShapeDtypeStruct((128, 128), BF16),
            jax.ShapeDtypeStruct((128, 768), BF16),
            jax.ShapeDtypeStruct((1, 768), F32),
            jax.ShapeDtypeStruct((4, 16, 128), F32),
        ),
        in_specs=[hbm] * 12 + [smem] * 2,
        out_specs=(vmem,) * 5,
        scratch_shapes=[
            pltpu.VMEM((N, 2, 4, 16, 512), BF16),
            pltpu.VMEM((4, 64, 128), F32),
            pltpu.VMEM((4, 64, 128), F32),
            pltpu.VMEM((64, 216), BF16),
            pltpu.VMEM((1, 64), BF16),
            pltpu.VMEM((1, 64), BF16),
            pltpu.VMEM((TAPS, 16, 64), BF16),
            pltpu.VMEM((1, 16), F32),
            pltpu.VMEM((64, 256), BF16),
            pltpu.VMEM((24, 128), BF16),
            pltpu.VMEM((48, 768), BF16),
            pltpu.VMEM((6, 128), BF16),
            pltpu.VMEM((1, 128), BF16),
            pltpu.VMEM((1, 128), BF16),
            pltpu.VMEM((N, 2, 4, 64, 256), BF16),
            pltpu.VMEM((9, 192, 512), BF16),
            pltpu.VMEM((4, 64, 128), F32),
            pltpu.VMEM((144, 192), BF16),
            pltpu.VMEM((128, 512), BF16),
            pltpu.VMEM((64, 8, 128), F32),
            pltpu.VMEM((N, 8, 8, 128), F32),
            pltpu.VMEM((8, 8, 128), F32),
            pltpu.VMEM((N, 8, 128), F32),
            pltpu.VMEM((N, 8, 128), F32),
            pltpu.VMEM((N, 8, 8, 128), F32),
            pltpu.VMEM((N * N, 128), F32),
            pltpu.VMEM((N, 16, 256), F32),
            pltpu.VMEM((N, 16, 256), F32),
            pltpu.VMEM((2, 16, 128), F32),
            pltpu.VMEM((5, 16, 128), F32),
            pltpu.VMEM((N, 16, 128), BF16),
            dma((12,)),
            dma((4, 2)),
            dma((4, 2)),
            dma((3, 2)),
            dma((3, 2)),
            dma((2,)),
            dma((2,)),
            dma((4,)),
            dma((4,)),
            dma((N,)),
            dma((N,)),
            dma((N, 4)),
            dma((N, 4)),
            dma((N,)),
            dma((N,)),
            dma((4, N)),
            dma((4, N)),
            dma,
            dma,
            dma((N,)),
            dma((N,)),
            dma((5,)),
            dma((5,)),
            dma((N,)),
            dma((N,)),
        ],
        compiler_params=pltpu.CompilerParams(
            collective_id=0, has_side_effects=True, vmem_limit_bytes=63 * 2**20
        ),
    )(
        clip_inputs[0],
        conv_in_weight.T,
        group_gain[None],
        group_bias[None],
        conv_out_weight.transpose(0, 2, 1),
        out_bias[None],
        patch_weight,
        patch_bias.reshape(24, 128),
        qkv_weight,
        qkv_bias.reshape(6, 128),
        q_gain[None],
        k_gain[None],
        frame_pos,
        row_pos,
    )
    latents, queries, keys, values = pl.pallas_call(
        project,
        out_shape=(
            jax.ShapeDtypeStruct((1, 2, 2, 256), F32),
            jax.ShapeDtypeStruct((128, 256), BF16),
            jax.ShapeDtypeStruct((128, 256), BF16),
            jax.ShapeDtypeStruct((128, 256), BF16),
        ),
        in_specs=[vmem] * 5,
        out_specs=(vmem,) * 4,
    )(*travelled)
    merged = (N, 2, 1, 8, 2 * HD)
    return (
        latents,
        queries.reshape(merged),
        keys.reshape(merged),
        values.reshape(merged),
    )


def solution(mesh):
    placed = (
        P("dp", "tm", "height", None, None),
        P(("tm", "height"), "dp"),
        P("dp"),
        P("dp"),
        P(None, "dp", None),
        P(),
        P(),
        P(),
        P(("tm", "height"), "dp"),
        P("dp"),
        P(),
        P(),
        P("tm"),
        P("height"),
    )
    return jax.shard_map(
        shards,
        mesh=mesh,
        in_specs=placed,
        out_specs=(
            P("dp", "tm", "height", None),
            P(None, "tm", "height", None, "dp"),
            P(None, "tm", "height", None, "dp"),
            P(None, "tm", "height", None, "dp"),
        ),
        check_vma=False,
    )
```
